128 devices in a mesh: dp: 4 (over y_lo, core), ctx: 32 (over z, y_hi, x).
Axes of the slice: x: 4, y: 4 (y_hi: 2, y_lo: 2; y = y_hi * 2 + y_lo), z: 4, core: 2. Of those that a mesh axis runs over, the one named last changes fastest.
Arguments:
- normed_layer_input: bfloat16 [4, 6144, 8192], P('dp', 'ctx'), may hold values from -18 to 18
- query: bfloat16 [4, 6144, 8192], P('dp', 'ctx'), may hold values from -9 to 9
- saved_key_value: bfloat16 [4, 6144, 2048], P('dp', 'ctx'), may hold values from -12 to 12
- output_gradient: bfloat16 [4, 6144, 8192], P('dp', 'ctx'), may hold values from -6 to 6
- adapter_down_weight: bfloat16 [24, 8192], replicated, may hold values from -0.0625 to 0.0625
- adapter_up_weight: bfloat16 [8, 10240], replicated, may hold values from -0.09375 to 0.09375
- shifted_head_flags: int32 [8], replicated, may hold values from 0 to 1, as said below
Outputs:
- grad_proj: bfloat16 [4, 6144, 10240], P('dp', 'ctx')
- grad_down: float32 [24, 8192], P(None, 'ctx')
- grad_up: float32 [8, 10240], P(None, 'ctx')
- grad_norm: float32 [], replicated
The draws below stay inside these ranges and needn't reach their ends.
Inputs may be any that keep to these rules, and one draw needn't show every extreme that they name: `shifted_head_flags`: exactly 4 entries are 1, the others 0.
All inputs are finite; a program needn't handle non-finite values.
Results may differ from the reference program's by a relative error of at most 0.0067.
Values may be sent and summed in bfloat16 or wider, within the bound.
A program may use at most 128 MiB of HBM per device.

```python
import math
import jax
import jax.numpy as jnp
from jax import lax

MODEL_WIDTH = 8192
HQ = 64
KVH = 8
HD = 128
ADAPTER_RANK = 8
DQ = 8192
DKV = 1024
QKV_COLUMNS = 10240
BATCH = 4
SEQ = 6144
GROUP = 768


def draw_query(key, part):
    mine = jax.random.fold_in(key, 11)
    shape = (BATCH, SEQ, HQ, HD)
    values = jax.random.truncated_normal(mine, -6.0, 6.0, shape, jnp.float32)
    return values.reshape(BATCH, SEQ, HQ * HD).astype(jnp.bfloat16)


def draw_saved_key_value(key, part):
    mine = jax.random.fold_in(key, 12)
    first, second = jax.random.split(mine, 2)
    shape = (BATCH, SEQ, KVH, HD)
    keys = jax.random.truncated_normal(first, -6.0, 6.0, shape, jnp.float32)
    values = jax.random.truncated_normal(second, -6.0, 6.0, shape, jnp.float32)
    joined = jnp.concatenate([keys.reshape(BATCH, SEQ, KVH * HD), values.reshape(BATCH, SEQ, KVH * HD)], axis=-1)
    return joined.astype(jnp.bfloat16)


def draw_normed_layer_input(key, part):
    mine = jax.random.fold_in(key, 13)
    shape = (BATCH, SEQ, MODEL_WIDTH)
    ramp = 3.0 ** (jnp.arange(MODEL_WIDTH).astype(jnp.float32) / MODEL_WIDTH)
    values = jax.random.truncated_normal(mine, -6.0, 6.0, shape, jnp.float32) * ramp
    return values.astype(jnp.bfloat16)


def draw_shifted_head_flags(key, part):
    mine = jax.random.fold_in(key, 14)
    order = jax.random.permutation(mine, KVH)
    return (order < KVH // 2).astype(jnp.int32)


def levels(key, extent, cuts, least, largest):
    def one(position, parts):
        steps = jax.random.uniform(jax.random.fold_in(jax.random.fold_in(key, 6), position), (parts,), jnp.float32, least / len(cuts), largest / len(cuts))
        return jnp.repeat(jnp.exp(steps), extent[position] // parts).reshape((-1,) + (1,) * (len(extent) - position - 1))

    gain = one(*cuts[0])
    for cut in cuts[1:]:
        gain = gain * one(*cut)
    return gain


def centred(rng, extent, scale, limit, shards=(), kind=jnp.bfloat16):
    result = scale * jax.random.normal(rng, extent, jnp.float32)
    if shards:
        result = result * levels(rng, extent, shards, -0.22, 0.18)
    return jnp.clip(result, -limit, limit).astype(kind)


def setup_inputs(seed: int = 0) -> dict:
    splits = jax.random.split(jax.random.key(seed), 8)
    normed_layer_input = draw_normed_layer_input(jax.random.fold_in(splits[7], 71), 0)
    query = draw_query(jax.random.fold_in(splits[7], 71), 0)
    saved_key_value = draw_saved_key_value(jax.random.fold_in(splits[7], 71), 0)
    output_gradient = centred(splits[3], (BATCH, SEQ, DQ), 1.0, 6.0, ((0, 4), (1, 32)))
    adapter_down_weight = centred(splits[4], (3 * ADAPTER_RANK, MODEL_WIDTH), MODEL_WIDTH ** -0.5, 0.0625)
    adapter_up_weight = centred(splits[5], (ADAPTER_RANK, QKV_COLUMNS), (ADAPTER_RANK * 512) ** -0.5, 0.09375)
    shifted_head_flags = draw_shifted_head_flags(jax.random.fold_in(splits[7], 71), 0)
    return {"normed_layer_input": normed_layer_input, "query": query, "saved_key_value": saved_key_value, "output_gradient": output_gradient, "adapter_down_weight": adapter_down_weight, "adapter_up_weight": adapter_up_weight, "shifted_head_flags": shifted_head_flags}


rope_base = 10000.0
adapter_scale = 2.0

def rotary_tables(positions):
    freqs = jnp.exp(jnp.arange(HD // 2, dtype=jnp.float32) * (-2.0 * math.log(rope_base) / HD))
    angles = positions[:, None] * freqs[None, :]
    return (jnp.cos(angles), jnp.sin(angles))

def rotary_back(grads, cosines, sines):
    first = grads[..., :HD // 2]
    second = grads[..., HD // 2:]
    cosine = cosines[:, None, :]
    sine = sines[:, None, :]
    return jnp.concatenate([first * cosine + second * sine, second * cosine - first * sine], axis=-1)

def group_backward(packed):
    query_group, key_group, value_group, grad_group = packed
    scale = HD ** (-0.5)
    query_wide = query_group.astype(jnp.float32)
    key_wide = key_group.astype(jnp.float32)
    scores = jnp.einsum('ihd,jd->hij', query_wide, key_wide) * scale
    rows_pos = jnp.arange(GROUP)[:, None]
    cols_pos = jnp.arange(GROUP)[None, :]
    allowed = (cols_pos <= rows_pos)[None]
    masked = jnp.where(allowed, scores, -1e+30)
    peak = lax.optimization_barrier(jnp.max(masked, axis=-1, keepdims=True))
    weights = jnp.exp(masked - peak)
    probs = weights / lax.optimization_barrier(jnp.sum(weights, axis=-1, keepdims=True))
    probs_low = lax.optimization_barrier(probs.astype(jnp.bfloat16)).astype(jnp.float32)
    grad_wide = grad_group.astype(jnp.float32)
    grad_value = jnp.einsum('hij,ihd->jd', probs_low, grad_wide)
    grad_probs = jnp.einsum('ihd,jd->hij', grad_wide, value_group.astype(jnp.float32))
    inner = lax.optimization_barrier(jnp.sum(probs * grad_probs, axis=-1, keepdims=True))
    grad_scores = lax.optimization_barrier((probs * (grad_probs - inner)).astype(jnp.bfloat16)).astype(jnp.float32)
    grad_query = jnp.einsum('hij,jd->ihd', grad_scores, key_wide) * scale
    grad_key = jnp.einsum('hij,ihd->jd', grad_scores, query_wide) * scale
    return (grad_query, grad_key, grad_value)

def sequence_head(query_head, key_head, value_head, grad_head, flag):
    half = GROUP // 2
    count = SEQ // GROUP

    def roll_in(array):
        return jnp.where(flag > 0, jnp.roll(array, -half, axis=0), array)

    def roll_out(array):
        return jnp.where(flag > 0, jnp.roll(array, half, axis=0), array)
    group_heads = HQ // KVH
    stacked = (roll_in(query_head).reshape(count, GROUP, group_heads, HD), roll_in(key_head).reshape(count, GROUP, HD), roll_in(value_head).reshape(count, GROUP, HD), roll_in(grad_head).reshape(count, GROUP, group_heads, HD))
    grad_query, grad_key, grad_value = lax.map(group_backward, stacked)
    return (roll_out(grad_query.reshape(SEQ, group_heads, HD)), roll_out(grad_key.reshape(SEQ, HD)), roll_out(grad_value.reshape(SEQ, HD)))

def reference(normed_layer_input, query, saved_key_value, output_gradient, adapter_down_weight, adapter_up_weight, shifted_head_flags):
    group_heads = HQ // KVH
    cosines, sines = rotary_tables(jnp.arange(SEQ).astype(jnp.float32))
    projected = []
    for batch_row in range(BATCH):
        queries = query[batch_row].reshape(SEQ, KVH, group_heads, HD)
        keys = saved_key_value[batch_row][:, :DKV].reshape(SEQ, KVH, HD)
        values = saved_key_value[batch_row][:, DKV:].reshape(SEQ, KVH, HD)
        grads = output_gradient[batch_row].reshape(SEQ, KVH, group_heads, HD)
        query_parts, key_parts, value_parts = ([], [], [])
        for head in range(KVH):
            part_query, part_key, part_value = sequence_head(queries[:, head], keys[:, head], values[:, head], grads[:, head], shifted_head_flags[head])
            query_parts.append(part_query)
            key_parts.append(part_key)
            value_parts.append(part_value)
        grad_query = jnp.stack(query_parts, axis=1).reshape(SEQ, HQ, HD)
        grad_key = jnp.stack(key_parts, axis=1)
        grad_value = jnp.stack(value_parts, axis=1)
        grad_query = rotary_back(grad_query, cosines, sines)
        grad_key = rotary_back(grad_key, cosines, sines)
        projected.append(jnp.concatenate([grad_query.reshape(SEQ, DQ), grad_key.reshape(SEQ, DKV), grad_value.reshape(SEQ, DKV)], axis=-1).astype(jnp.bfloat16))
    grad_proj = jnp.stack(projected, axis=0)
    flattened_inputs = normed_layer_input.reshape(BATCH * SEQ, MODEL_WIDTH)
    flat_grads = grad_proj.reshape(BATCH * SEQ, QKV_COLUMNS)
    down_reduced = jnp.dot(flattened_inputs, adapter_down_weight.T, preferred_element_type=jnp.float32).astype(jnp.bfloat16)
    edges = [(0, DQ), (DQ, DKV), (DQ + DKV, DKV)]
    up_pieces_list, down_pieces_list = ([], [])
    for segment, (column_offset, piece_width) in enumerate(edges):
        gradient_piece = flat_grads[:, column_offset:column_offset + piece_width]
        reduced_piece = down_reduced[:, segment * ADAPTER_RANK:(segment + 1) * ADAPTER_RANK]
        up_pieces_list.append(adapter_scale * jnp.dot(reduced_piece.T, gradient_piece, preferred_element_type=jnp.float32))
        blended_product = jnp.dot(gradient_piece, adapter_up_weight[:, column_offset:column_offset + piece_width].T, preferred_element_type=jnp.float32).astype(jnp.bfloat16)
        down_pieces_list.append(adapter_scale * jnp.dot(blended_product.T, flattened_inputs, preferred_element_type=jnp.float32))
    grad_down = jnp.concatenate(down_pieces_list, axis=0)
    grad_up = jnp.concatenate(up_pieces_list, axis=1)
    grad_norm = jnp.sqrt(jnp.sum(grad_down * grad_down) + jnp.sum(grad_up * grad_up))
    return (grad_proj, grad_down, grad_up, grad_norm)
```

```python
import functools
import math

import jax
import jax.numpy as jnp
from jax import lax
from jax.experimental import pallas as pl
from jax.experimental.pallas import tpu as pltpu
from jax.sharding import PartitionSpec as P

HQ = 64
KVH = 8
HD = 128
HALF = KVH // 2
GROUP_HEADS = HQ // KVH
ADAPTER_RANK = 8
GROUP_DEV = 4
PACK = 4

rope_base = 10000.0
adapter_scale = 2.0
SCALE = HD ** (-0.5)
SCALE_LOG2 = SCALE * math.log2(math.e)
MESH = pl.DeviceIdType.MESH
VMEM = pl.BlockSpec(memory_space=pltpu.VMEM)
SMEM = pl.BlockSpec(memory_space=pltpu.SMEM)
ANY = pl.BlockSpec(memory_space=pl.ANY)
F32 = jnp.float32
BF16 = jnp.bfloat16


def head_order(flags):
    heads = jnp.arange(KVH)
    shifted = (flags > 0).astype(jnp.int32)
    before = heads[None, :] < heads[:, None]
    ones_before = jnp.sum(jnp.where(before, shifted[None, :], 0), axis=1)
    place = jnp.where(shifted > 0, HALF + ones_before, heads - ones_before)
    return jnp.sum(jnp.where(place[None, :] == heads[:, None], heads[None, :], 0), axis=1)


def dot(a, b, ca, cb):
    return lax.dot_general(a, b, (((ca,), (cb,)), ((), ())), preferred_element_type=F32)


def attention_kernel(
    order,
    q_hbm,
    g_hbm,
    kv_hbm,
    cosines,
    sines,
    dq_hbm,
    dkv,
    kv,
    qv,
    gv,
    window,
    staged,
    returned,
    own,
    dqs,
    kv_sem,
    in_sem,
    out_sem,
    fsend,
    frecv,
    bsend,
    brecv,
):
    rows = q_hbm.shape[0]
    dp = lax.axis_index("dp")
    place = lax.axis_index("ctx")
    count = lax.axis_size("ctx")
    odd = lax.rem(place, 2)
    first = lax.rem(place, GROUP_DEV)
    second = lax.rem(place + 2, GROUP_DEV)
    low_base = jnp.where(first < 2, 0, HALF)
    high_base = HALF - low_base
    width = GROUP_HEADS * HD
    kv_in = [
        pltpu.make_async_copy(kv_hbm.at[:, h * HD : (h + 1) * HD], kv.at[h], kv_sem.at[h])
        for h in range(2 * KVH)
    ]
    copies_in = []
    for h in range(KVH):
        part = slice(h * width, (h + 1) * width)
        copies_in.append(pltpu.make_async_copy(q_hbm.at[:, part], qv.at[h], in_sem.at[0, h]))
        copies_in.append(pltpu.make_async_copy(g_hbm.at[:, part], gv.at[h], in_sem.at[1, h]))
    for copy in kv_in + copies_in:
        copy.start()

    def peer(offset):
        return (dp, lax.rem(place + offset + count, count))

    barrier = pltpu.get_barrier_semaphore()
    for rank in (first, second):
        for step in range(1, GROUP_DEV):
            mate = lax.rem(rank + step, GROUP_DEV)
            pl.semaphore_signal(barrier, inc=1, device_id=peer(mate - rank), device_id_type=MESH)

    for copy in kv_in:
        copy.wait()
    for c in range(KVH):
        rank = first if c < HALF else second
        head = order[c]
        slot = pl.ds(pl.multiple_of(rank * rows, rows), rows)
        window[c, slot, 0:HD] = kv[head]
        window[c, slot, HD : 2 * HD] = kv[head + KVH]

    pl.semaphore_wait(barrier, 2 * (GROUP_DEV - 1))

    def forward(c, rank, distance):
        part = window.at[c, rank * rows : (rank + 1) * rows]
        return pltpu.make_async_remote_copy(
            src_ref=part,
            dst_ref=part,
            send_sem=fsend.at[c, distance - 1],
            recv_sem=frecv.at[c, rank],
            device_id=peer(distance),
            device_id_type=MESH,
        )

    def back(c, rank, target):
        return pltpu.make_async_remote_copy(
            src_ref=staged.at[c, target],
            dst_ref=returned.at[c, rank - 1],
            send_sem=bsend.at[c, target],
            recv_sem=brecv.at[c, rank - 1],
            device_id=peer(target - rank),
            device_id_type=MESH,
        )

    def each_head(step):
        lax.fori_loop(0, HALF, lambda i, _: (step(i), 0)[1], 0)

    def work(c, rank):
        blocks = rank + 1
        span = blocks * rows
        for source in range(rank):
            forward(c, source, rank - source).wait_recv()
        head = order[c]
        keys = window[c, 0:span, 0:HD]
        values = window[c, 0:span, HD : 2 * HD]
        width = PACK * rows
        row = lax.broadcasted_iota(jnp.int32, (rows, width), 0)
        column = lax.rem(lax.broadcasted_iota(jnp.int32, (rows, width), 1), rows)
        allowed = row <= column
        key_sum, value_sum = None, None
        for j in range(GROUP_HEADS // PACK):

            def stacked(ref):
                return jnp.concatenate(
                    [ref[head, :, (j * PACK + t) * HD : (j * PACK + t + 1) * HD] for t in range(PACK)],
                    axis=0,
                )

            queries = stacked(qv)
            grads = stacked(gv)
            scores = dot(keys, queries, 1, 1)
            grad_probs = dot(values, grads, 1, 1)
            last = jnp.where(allowed, scores[span - rows :], -1e30)
            scores = jnp.concatenate([scores[: span - rows], last], axis=0) if rank else last
            peak = jnp.max(scores, axis=0, keepdims=True)
            weights = jnp.exp2((scores - peak) * SCALE_LOG2)
            probs = weights * (1.0 / jnp.sum(weights, axis=0, keepdims=True))
            inner = jnp.sum(probs * grad_probs, axis=0, keepdims=True)
            probs_low = probs.astype(BF16)
            grad_scores = (probs * (grad_probs - inner)).astype(BF16)
            value_term = dot(probs_low, grads, 1, 0)
            key_term = dot(grad_scores, queries, 1, 0)
            value_sum = value_term if value_sum is None else value_sum + value_term
            key_sum = key_term if key_sum is None else key_sum + key_term
            grad_query = dot(grad_scores, keys, 0, 0)
            for t in range(PACK):
                piece = grad_query[t * rows : (t + 1) * rows]
                piece = piece * cosines[...] + pltpu.roll(piece, HD // 2, 1) * sines[...]
                lanes = (j * PACK + t) * HD
                dqs[c, :, lanes : lanes + HD] = piece.astype(BF16)
        pltpu.make_async_copy(dqs.at[c], dq_hbm.at[c], out_sem.at[c]).start()
        for target in range(rank):
            part = slice(target * rows, (target + 1) * rows)
            staged[c, target, :, 0:HD] = key_sum[part].astype(BF16)
            staged[c, target, :, HD : 2 * HD] = value_sum[part].astype(BF16)
            back(c, rank, target).start()
        own[c, :, 0:HD] = key_sum[span - rows :]
        own[c, :, HD : 2 * HD] = value_sum[span - rows :]

    def finish(c, rank):
        total = own[c]
        for sender in range(rank + 1, GROUP_DEV):
            back(c, sender, rank).wait_recv()
            total = total + returned[c, sender - 1].astype(F32)
        keys = total[:, 0:HD]
        keys = keys * cosines[...] + pltpu.roll(keys, HD // 2, 1) * sines[...]
        dkv[c, :, 0:HD] = keys.astype(BF16)
        dkv[c, :, HD : 2 * HD] = total[:, HD : 2 * HD].astype(BF16)

    def phase(low, high):
        sends = [(low_base, low, d) for d in range(1, GROUP_DEV - low)]
        sends += [(high_base, high, d) for d in range(1, GROUP_DEV - high)]
        if low == 0:
            each_head(lambda i: forward(low_base + i, low, 1).start())
            sends = sends[1:]

        def send_all(i):
            for base, rank, distance in sends:
                forward(base + i, rank, distance).start()

        each_head(send_all)
        for copy in copies_in:
            copy.wait()
        each_head(lambda i: work(low_base + i, low))
        each_head(lambda i: work(high_base + i, high))

        def last(i):
            finish(high_base + i, high)
            finish(low_base + i, low)

        each_head(last)

        def drain(i):
            for base, rank in ((low_base, low), (high_base, high)):
                for distance in range(1, GROUP_DEV - rank):
                    forward(base + i, rank, distance).wait_send()
                for target in range(rank):
                    back(base + i, rank, target).wait_send()
                c = base + i
                pltpu.make_async_copy(dqs.at[c], dq_hbm.at[c], out_sem.at[c]).wait()

        each_head(drain)

    pl.when(odd == 0)(lambda: phase(0, 2))
    pl.when(odd == 1)(lambda: phase(1, 3))


def attention(order, query, grads, kv, cosines, sines):
    rows = query.shape[0]
    width = GROUP_HEADS * HD
    return pl.pallas_call(
        attention_kernel,
        out_shape=(
            jax.ShapeDtypeStruct((KVH, rows, width), BF16),
            jax.ShapeDtypeStruct((KVH, rows, 2 * HD), BF16),
        ),
        in_specs=[SMEM, ANY, ANY, ANY, VMEM, VMEM],
        out_specs=(ANY, VMEM),
        scratch_shapes=[
            pltpu.VMEM((2 * KVH, rows, HD), BF16),
            pltpu.VMEM((KVH, rows, width), BF16),
            pltpu.VMEM((KVH, rows, width), BF16),
            pltpu.VMEM((KVH, GROUP_DEV * rows, 2 * HD), BF16),
            pltpu.VMEM((KVH, GROUP_DEV - 1, rows, 2 * HD), BF16),
            pltpu.VMEM((KVH, GROUP_DEV - 1, rows, 2 * HD), BF16),
            pltpu.VMEM((KVH, rows, 2 * HD), F32),
            pltpu.VMEM((KVH, rows, width), BF16),
            pltpu.SemaphoreType.DMA((2 * KVH,)),
            pltpu.SemaphoreType.DMA((2, KVH)),
            pltpu.SemaphoreType.DMA((KVH,)),
            pltpu.SemaphoreType.DMA((KVH, GROUP_DEV - 1)),
            pltpu.SemaphoreType.DMA((KVH, GROUP_DEV - 1)),
            pltpu.SemaphoreType.DMA((KVH, GROUP_DEV - 1)),
            pltpu.SemaphoreType.DMA((KVH, GROUP_DEV - 1)),
        ],
        compiler_params=pltpu.CompilerParams(
            collective_id=0, has_side_effects=True, vmem_limit_bytes=52 * 2**20
        ),
        name="attention_backward",
    )(order, query, grads, kv, cosines, sines)


SHARDS = 32
PIECE = 48
RING = 4


def packed_place(shard):
    z, rest = divmod(shard, 8)
    high, x = divmod(rest, 4)
    return (z * 4 + x) * 2 + high


def adapter_kernel(
    order, x_hbm, dq_hbm, dkv, down_w, up_w, out_hbm, packed, xv, dqv, kvn, up, x_sem, dq_sem, out_sem
):
    width = GROUP_HEADS * HD
    width_q = HQ * HD
    width_kv = KVH * HD
    rank = ADAPTER_RANK
    x_copy = pltpu.make_async_copy(x_hbm, xv, x_sem)
    x_copy.start()

    def dq_copy(c):
        return pltpu.make_async_copy(dq_hbm.at[c], dqv.at[c], dq_sem.at[c])

    def out_copy(c):
        columns = pl.ds(pl.multiple_of(order[c] * width, width), width)
        return pltpu.make_async_copy(dqv.at[c], out_hbm.at[:, columns], out_sem.at[c])

    for c in range(KVH):
        dq_copy(c).start()
    for c in range(KVH):
        head = order[c]
        kvn[:, pl.ds(pl.multiple_of(head * HD, HD), HD)] = dkv[c, :, 0:HD]
        kvn[:, pl.ds(pl.multiple_of((head + KVH) * HD, HD), HD)] = dkv[c, :, HD : 2 * HD]
    kv_copy = pltpu.make_async_copy(
        kvn, out_hbm.at[:, width_q : width_q + 2 * width_kv], out_sem.at[KVH]
    )
    kv_copy.start()
    x_copy.wait()
    low = jnp.transpose(dot(xv[...], down_w[...], 1, 1)).astype(BF16)
    low_q, low_k, low_v = (low[s * rank : (s + 1) * rank] for s in range(3))
    mixed_q = None
    for c in range(KVH):
        dq_copy(c).wait()
        out_copy(c).start()
        columns = pl.ds(pl.multiple_of(order[c] * width, width), width)
        up[:, columns] = adapter_scale * dot(low_q, dqv[c], 1, 0)
        term = dot(dqv[c], up_w[:, columns], 1, 1)
        mixed_q = term if mixed_q is None else mixed_q + term
    up[:, width_q : width_q + width_kv] = adapter_scale * dot(low_k, kvn[:, 0:width_kv], 1, 0)
    up[:, width_q + width_kv :] = adapter_scale * dot(low_v, kvn[:, width_kv:], 1, 0)
    mixed_k = dot(kvn[:, 0:width_kv], up_w[:, width_q : width_q + width_kv], 1, 1)
    mixed_v = dot(kvn[:, width_kv:], up_w[:, width_q + width_kv :], 1, 1)
    mixed = jnp.transpose(jnp.concatenate([mixed_q, mixed_k, mixed_v], axis=1)).astype(BF16)
    down_width = xv.shape[1] // SHARDS
    up_width = up.shape[1] // SHARDS
    zeros = jnp.zeros((8, HD), F32)
    for shard in range(SHARDS):
        down = adapter_scale * dot(mixed, xv[:, shard * down_width : (shard + 1) * down_width], 1, 0)
        mine = up[:, shard * up_width : (shard + 1) * up_width]
        rest = jnp.concatenate(
            [mine[:, 2 * HD :], jnp.zeros((8, 3 * HD - up_width), F32)], axis=1
        )
        at = packed_place(shard)
        packed[0, at] = jnp.concatenate([down[:, 0:HD], mine[:, 0:HD], rest, zeros], 0).astype(BF16)
        packed[1, at] = jnp.concatenate(
            [down[:, HD:], mine[:, HD : 2 * HD], zeros, zeros], 0
        ).astype(BF16)
    for c in range(KVH):
        out_copy(c).wait()
    kv_copy.wait()


def adapters(order, x, dq, dkv, down_w, up_w):
    rows, model = x.shape
    columns = up_w.shape[1]
    return pl.pallas_call(
        adapter_kernel,
        out_shape=(
            jax.ShapeDtypeStruct((rows, columns), BF16),
            jax.ShapeDtypeStruct((2, SHARDS, PIECE, HD), BF16),
        ),
        in_specs=[SMEM, ANY, ANY, VMEM, VMEM, VMEM],
        out_specs=(ANY, VMEM),
        scratch_shapes=[
            pltpu.VMEM((rows, model), BF16),
            pltpu.VMEM(dq.shape, BF16),
            pltpu.VMEM((rows, 2 * KVH * HD), BF16),
            pltpu.VMEM((ADAPTER_RANK, columns), F32),
            pltpu.SemaphoreType.DMA,
            pltpu.SemaphoreType.DMA((KVH,)),
            pltpu.SemaphoreType.DMA((KVH + 1,)),
        ],
        compiler_params=pltpu.CompilerParams(vmem_limit_bytes=48 * 2**20),
        name="adapter_terms",
    )(order, x, dq, dkv, down_w, up_w)


def reduce_kernel(
    packed,
    down_out,
    up_out,
    norm_out,
    got1,
    sum1,
    got2,
    sum2,
    got3,
    halves,
    norms,
    quarters,
    send1,
    recv1,
    send2,
    recv2,
    send3,
    recv3,
    send4,
    recv4,
    send5,
    recv5,
    send6,
    recv6,
):
    dp = lax.axis_index("dp")
    place = lax.axis_index("ctx")
    core = lax.rem(dp, 2)
    y_low = lax.div(dp, 2)
    z = lax.div(place, 8)
    y_high = lax.rem(lax.div(place, 4), 2)
    x = lax.rem(place, 4)
    y = y_high * 2 + y_low
    plane = z * 4 + x

    def device(plane, y, core):
        high, low = lax.div(y, 2), lax.rem(y, 2)
        return (low * 2 + core, lax.div(plane, 4) * 8 + high * 4 + lax.rem(plane, 4))

    def remote(src, dst, send, recv, target):
        return pltpu.make_async_remote_copy(
            src_ref=src,
            dst_ref=dst,
            send_sem=send,
            recv_sem=recv,
            device_id=target,
            device_id_type=MESH,
        )

    def in_plane(step):
        return lax.rem(plane + step, 16)

    def in_ring(step):
        return lax.rem(y + step, RING)

    def quarter_device(step):
        code = lax.rem(core * 2 + y_high + step, 4)
        return device(plane, lax.rem(code, 2) * 2 + y_low, lax.div(code, 2))

    mate = device(plane, y, 1 - core)
    barrier = pltpu.get_barrier_semaphore()

    def greet(target):
        pl.semaphore_signal(barrier, inc=1, device_id=target, device_id_type=MESH)

    greet(mate)
    lax.fori_loop(1, 16, lambda k, _: (greet(device(in_plane(k), y, core)), 0)[1], 0)
    for step in range(1, RING):
        greet(device(plane, in_ring(step), core))
        greet(quarter_device(step))
    pl.semaphore_wait(barrier, 1 + 15 + 2 * (RING - 1))

    first = remote(packed.at[1 - core], got1, send1, recv1, mate)
    first.start()
    first.wait_recv()

    def both(t):
        part = pl.ds(2 * t, 2)
        return packed[core, part].astype(F32) + got1[part].astype(F32)

    def second(k):
        t = in_plane(k)
        part = pl.ds(2 * t, 2)
        return remote(
            sum1.at[part], got2.at[plane], send2.at[k], recv2.at[plane], device(t, y, core)
        )

    def send_second(k, _):
        t = in_plane(k)
        sum1[pl.ds(2 * t, 2)] = both(t).astype(BF16)
        second(k).start()
        return 0

    lax.fori_loop(1, 16, send_second, 0)
    total = both(plane)

    def add_second(k, total):
        source = in_plane(16 - k)
        remote(
            sum1.at[pl.ds(0, 2)], got2.at[source], send2.at[k], recv2.at[source], mate
        ).wait_recv()
        return total + got2[source].astype(F32)

    sum2[...] = lax.fori_loop(1, 16, add_second, total)

    def third(step):
        target = in_ring(step)
        return remote(
            sum2.at[lax.div(target, 2)],
            got3.at[y],
            send3.at[step],
            recv3.at[y],
            device(plane, target, core),
        )

    for step in range(1, RING):
        third(step).start()
    got3[y] = sum2[y_high]
    for step in range(1, RING):
        source = in_ring(step)
        remote(sum2.at[0], got3.at[source], send3.at[step], recv3.at[source], mate).wait_recv()
    mine = got3[0] + got3[1] + got3[2] + got3[3]
    halves[core] = mine
    fourth = remote(halves.at[core], halves.at[core], send4, recv4, mate)
    fourth.start()
    squares = mine * mine
    norms[plane] = functools.reduce(
        lambda a, b: a + b, [squares[8 * r : 8 * (r + 1)] for r in range(PIECE // 8)]
    )

    def fifth(k):
        return remote(
            norms.at[plane], norms.at[plane], send5.at[k], recv5.at[plane], device(in_plane(k), y, core)
        )

    def fifth_arrival(k):
        source = in_plane(k)
        return remote(norms.at[source], norms.at[source], send5.at[k], recv5.at[source], mate)

    lax.fori_loop(1, 16, lambda k, _: (fifth(k).start(), 0)[1], 0)
    lax.fori_loop(1, 16, lambda k, _: (fifth_arrival(k).wait_recv(), 0)[1], 0)
    code = core * 2 + y_high
    quarters[code] = jnp.sum(norms[...], axis=0)

    def sixth(step):
        return remote(
            quarters.at[code], quarters.at[code], send6.at[step], recv6.at[code], quarter_device(step)
        )

    for step in range(1, 4):
        sixth(step).start()
    remote(halves.at[core], halves.at[1 - core], send4, recv4, mate).wait_recv()
    down_out[:, 0:HD] = halves[0, 0:24]
    down_out[:, HD : 2 * HD] = halves[1, 0:24]
    up_out[:, 0:HD] = halves[0, 24:32]
    up_out[:, HD : 2 * HD] = halves[1, 24:32]
    up_out[:, 2 * HD :] = halves[0, 32:40, 0 : up_out.shape[1] - 2 * HD]
    for step in range(1, 4):
        source = lax.rem(code + step, 4)
        remote(
            quarters.at[source], quarters.at[source], send6.at[step], recv6.at[source], mate
        ).wait_recv()
    everything = jnp.sum(jnp.sum(quarters[...], axis=0), keepdims=True)
    norm_out[...] = jnp.broadcast_to(jnp.sqrt(everything), norm_out.shape)

    first.wait_send()
    fourth.wait_send()
    lax.fori_loop(1, 16, lambda k, _: (second(k).wait_send(), 0)[1], 0)
    lax.fori_loop(1, 16, lambda k, _: (fifth(k).wait_send(), 0)[1], 0)
    for step in range(1, 4):
        third(step).wait_send()
        sixth(step).wait_send()


def reduced(packed):
    dma = pltpu.SemaphoreType.DMA
    return pl.pallas_call(
        reduce_kernel,
        out_shape=(
            jax.ShapeDtypeStruct((24, 256), F32),
            jax.ShapeDtypeStruct((8, 320), F32),
            jax.ShapeDtypeStruct((8, HD), F32),
        ),
        in_specs=[VMEM],
        out_specs=(VMEM, VMEM, VMEM),
        scratch_shapes=[
            pltpu.VMEM((SHARDS, PIECE, HD), BF16),
            pltpu.VMEM((SHARDS, PIECE, HD), BF16),
            pltpu.VMEM((16, 2, PIECE, HD), BF16),
            pltpu.VMEM((2, PIECE, HD), F32),
            pltpu.VMEM((RING, PIECE, HD), F32),
            pltpu.VMEM((2, PIECE, HD), F32),
            pltpu.VMEM((16, 8, HD), F32),
            pltpu.VMEM((4, 8, HD), F32),
            dma,
            dma,
            dma((16,)),
            dma((16,)),
            dma((RING,)),
            dma((RING,)),
            dma,
            dma,
            dma((16,)),
            dma((16,)),
            dma((4,)),
            dma((4,)),
        ],
        compiler_params=pltpu.CompilerParams(
            collective_id=1, has_side_effects=True, vmem_limit_bytes=32 * 2**20
        ),
        name="adapter_sums",
    )(packed)


def rotary_tables(positions):
    freqs = jnp.exp(jnp.arange(HD // 2, dtype=F32) * (-2.0 * math.log(rope_base) / HD))
    angles = positions[:, None] * freqs[None, :]
    return (jnp.cos(angles), jnp.sin(angles))


def local(
    normed_layer_input,
    query,
    saved_key_value,
    output_gradient,
    adapter_down_weight,
    adapter_up_weight,
    shifted_head_flags,
):
    rows = query.shape[1]
    place = lax.axis_index("ctx")
    positions = (place * rows + jnp.arange(rows)).astype(F32)
    cosines, sines = rotary_tables(positions)
    cosines = jnp.concatenate([cosines, cosines], axis=1) * SCALE
    sines = jnp.concatenate([sines, -sines], axis=1) * SCALE
    order = head_order(shifted_head_flags)
    dq, dkv = attention(
        order, query[0], output_gradient[0], saved_key_value[0], cosines, sines
    )
    grad_proj, packed = adapters(
        order, normed_layer_input[0], dq, dkv, adapter_down_weight, adapter_up_weight
    )
    grad_down, grad_up, norm = reduced(packed)
    return (grad_proj[None], grad_down, grad_up, norm[0, 0])


def solution(mesh):
    return jax.shard_map(
        local,
        mesh=mesh,
        in_specs=(
            P("dp", "ctx", None),
            P("dp", "ctx", None),
            P("dp", "ctx", None),
            P("dp", "ctx", None),
            P(),
            P(),
            P(),
        ),
        out_specs=(P("dp", "ctx", None), P(None, "ctx"), P(None, "ctx"), P()),
        check_vma=False,
    )
```

```python
import functools
import math

import jax
import jax.numpy as jnp
import numpy as np
from jax import lax
from jax.experimental import pallas as pl
from jax.experimental.pallas import tpu as pltpu
from jax.sharding import PartitionSpec as P

HQ = 64
KVH = 8
HD = 128
HALF = KVH // 2
GROUP_HEADS = HQ // KVH
ADAPTER_RANK = 8
GROUP_DEV = 4
PACK = 4
SHARDS = 32
PIECE = 48
RING = 4
PLANE = 16

rope_base = 10000.0
adapter_scale = 2.0
SCALE = HD ** (-0.5)
SCALE_LOG2 = SCALE * math.log2(math.e)
MESH = pl.DeviceIdType.MESH
VMEM = pl.BlockSpec(memory_space=pltpu.VMEM)
SMEM = pl.BlockSpec(memory_space=pltpu.SMEM)
HBM = pl.BlockSpec(memory_space=pltpu.HBM)
F32 = jnp.float32
BF16 = jnp.bfloat16


def head_at(flags, position):
    ones = jnp.int32(0)
    head = jnp.int32(0)
    for h in range(KVH):
        flag = jnp.minimum(flags[h], 1)
        here = (1 - flag) * (h - ones) + flag * (HALF + ones)
        head = head + h * (here == position).astype(jnp.int32)
        ones = ones + flag
    return head


def positions_of(flags):
    ones = jnp.int32(0)
    found = []
    for h in range(KVH):
        flag = jnp.minimum(flags[h], 1)
        found.append((1 - flag) * (h - ones) + flag * (HALF + ones))
        ones = ones + flag
    return found


def dot(a, b, ca, cb):
    return lax.dot_general(a, b, (((ca,), (cb,)), ((), ())), preferred_element_type=F32)


def packed_place(shard):
    z, rest = divmod(shard, 8)
    high, x = divmod(rest, 4)
    return (z * 4 + x) * 2 + high


def kernel(
    flags,
    x_hbm,
    q_hbm,
    kv_hbm,
    g_hbm,
    down_w,
    up_w,
    row_table,
    block_table,
    grad_proj,
    down_out,
    up_out,
    norm_out,
    xv,
    kv,
    qv,
    gv,
    window,
    staged,
    returned,
    own,
    dqs,
    dkv,
    kvn,
    cosines,
    sines,
    low_t,
    up_heads,
    up,
    up_class,
    mixed_q,
    packed,
    got1,
    sum1,
    got2,
    sum2,
    got3,
    halves,
    norms,
    quarters,
    x_sem,
    kv_sem,
    in_sem,
    fsend,
    frecv,
    bsend,
    brecv,
    send1,
    recv1,
    send2,
    recv2,
    send3,
    recv3,
    send4,
    recv4,
    send5,
    recv5,
    send6,
    recv6,
):
    rows = q_hbm.shape[0]
    dp = lax.axis_index("dp")
    place = lax.axis_index("ctx")
    count = lax.axis_size("ctx")
    odd = lax.rem(place, 2)
    first_rank = lax.rem(place, GROUP_DEV)
    second_rank = lax.rem(place + 2, GROUP_DEV)
    low_base = jnp.where(first_rank < 2, 0, HALF)
    high_base = HALF - low_base
    core = lax.rem(dp, 2)
    y_low = lax.div(dp, 2)
    y_high = lax.rem(lax.div(place, 4), 2)
    y = y_high * 2 + y_low
    plane = lax.div(place, 8) * 4 + lax.rem(place, 4)
    width = GROUP_HEADS * HD
    width_q = HQ * HD
    width_kv = KVH * HD
    rank_a = ADAPTER_RANK

    kv_in = [
        pltpu.make_async_copy(kv_hbm.at[:, h * HD : (h + 1) * HD], kv.at[h], kv_sem.at[h])
        for h in range(2 * KVH)
    ]
    copies_in = []
    for h in range(KVH):
        part = slice(h * width, (h + 1) * width)
        copies_in.append(pltpu.make_async_copy(q_hbm.at[:, part], qv.at[h], in_sem.at[0, h]))
        copies_in.append(pltpu.make_async_copy(g_hbm.at[:, part], gv.at[h], in_sem.at[1, h]))
    x_in = pltpu.make_async_copy(x_hbm, xv, x_sem)
    for copy in kv_in + copies_in:
        copy.start()
    x_in.start()

    def peer(offset):
        return (dp, lax.rem(place + offset + count, count))

    def device(plane, y, core):
        high, low = lax.div(y, 2), lax.rem(y, 2)
        return (low * 2 + core, lax.div(plane, 4) * 8 + high * 4 + lax.rem(plane, 4))

    def in_plane(step):
        return lax.rem(plane + step, PLANE)

    def in_ring(step):
        return lax.rem(y + step, RING)

    def quarter_device(step):
        code = lax.rem(core * 2 + y_high + step, 4)
        return device(plane, lax.rem(code, 2) * 2 + y_low, lax.div(code, 2))

    mate = device(plane, y, 1 - core)
    barrier = pltpu.get_barrier_semaphore()

    def greet(target):
        pl.semaphore_signal(barrier, inc=1, device_id=target, device_id_type=MESH)

    for rank in (first_rank, second_rank):
        for step in range(1, GROUP_DEV):
            greet(peer(lax.rem(rank + step, GROUP_DEV) - rank))
    lax.fori_loop(1, PLANE, lambda k, _: (greet(device(in_plane(k), y, core)), 0)[1], 0)
    for step in range(1, RING):
        greet(device(plane, in_ring(step), core))
        greet(quarter_device(step))
    greet(mate)

    for copy in kv_in:
        copy.wait()
    for c in range(KVH):
        rank = first_rank if c < HALF else second_rank
        head = head_at(flags, c)
        slot = pl.ds(pl.multiple_of(rank * rows, rows), rows)
        window[c, slot, 0:HD] = kv[head]
        window[c, slot, HD : 2 * HD] = kv[head + KVH]

    pl.semaphore_wait(barrier, 2 * (GROUP_DEV - 1) + PLANE - 1 + 2 * (RING - 1) + 1)

    def forward(c, rank, distance):
        part = window.at[c, rank * rows : (rank + 1) * rows]
        return pltpu.make_async_remote_copy(
            src_ref=part,
            dst_ref=part,
            send_sem=fsend.at[c, distance - 1],
            recv_sem=frecv.at[c, rank],
            device_id=peer(distance),
            device_id_type=MESH,
        )

    def back(c, rank, target):
        return pltpu.make_async_remote_copy(
            src_ref=staged.at[c, target],
            dst_ref=returned.at[c, rank - 1],
            send_sem=bsend.at[c, target],
            recv_sem=brecv.at[c, rank - 1],
            device_id=peer(target - rank),
            device_id_type=MESH,
        )

    def each_head(step, start=0, stop=HALF):
        lax.fori_loop(start, stop, lambda i, _: (step(i), 0)[1], 0)

    def sends(low, high):
        if low == 0:
            each_head(lambda i: forward(low_base + i, 0, 1).start(), 0, 2)

        def send_all(i):
            for base, rank in ((low_base, low), (high_base, high)):
                for distance in range(2 if rank == 0 else 1, GROUP_DEV - rank):
                    forward(base + i, rank, distance).start()

        each_head(send_all)
        if low == 0:
            each_head(lambda i: forward(low_base + i, 0, 1).start(), 2, HALF)

    pl.when(odd == 0)(lambda: sends(0, 2))
    pl.when(odd == 1)(lambda: sends(1, 3))

    block_cos, block_sin = block_table[0, pl.ds(place, 1)], block_table[1, pl.ds(place, 1)]
    row_cos, row_sin = row_table[0], row_table[1]
    cosines[...] = block_cos * row_cos - block_sin * row_sin
    sines[...] = block_sin * row_cos + block_cos * row_sin
    for h in range(KVH):
        up_heads[h] = up_w[:, h * width : (h + 1) * width].astype(F32)
    mixed_q[...] = jnp.zeros_like(mixed_q)
    for copy in copies_in:
        copy.wait()
    x_in.wait()
    low_t[...] = jnp.transpose(dot(xv[...], down_w[...], 1, 1))

    def low_of(segment):
        return low_t[segment * rank_a : (segment + 1) * rank_a].astype(BF16)

    def work(c, rank):
        blocks = rank + 1
        span = blocks * rows
        for source in range(rank):
            forward(c, source, rank - source).wait_recv()
        head = head_at(flags, c)
        keys = window[c, 0:span, 0:HD]
        values = window[c, 0:span, HD : 2 * HD]
        packed_rows = PACK * rows
        row = lax.broadcasted_iota(jnp.int32, (rows, packed_rows), 0)
        column = lax.rem(lax.broadcasted_iota(jnp.int32, (rows, packed_rows), 1), rows)
        allowed = row <= column
        key_sum, value_sum = None, None
        for j in range(GROUP_HEADS // PACK):

            def stacked(ref):
                return jnp.concatenate(
                    [ref[head, :, (j * PACK + t) * HD : (j * PACK + t + 1) * HD] for t in range(PACK)],
                    axis=0,
                )

            queries = stacked(qv)
            grads = stacked(gv)
            scores = dot(keys, queries, 1, 1)
            grad_probs = dot(values, grads, 1, 1)
            last = jnp.where(allowed, scores[span - rows :], -1e30)
            scores = jnp.concatenate([scores[: span - rows], last], axis=0) if rank else last
            peak = jnp.max(scores, axis=0, keepdims=True)
            weights = jnp.exp2((scores - peak) * SCALE_LOG2)
            probs = weights * (1.0 / jnp.sum(weights, axis=0, keepdims=True))
            inner = jnp.sum(probs * grad_probs, axis=0, keepdims=True)
            probs_low = probs.astype(BF16)
            grad_scores = (probs * (grad_probs - inner)).astype(BF16)
            value_term = dot(probs_low, grads, 1, 0)
            key_term = dot(grad_scores, queries, 1, 0)
            value_sum = value_term if value_sum is None else value_sum + value_term
            key_sum = key_term if key_sum is None else key_sum + key_term
            grad_query = dot(grad_scores, keys, 0, 0)
            for t in range(PACK):
                piece = grad_query[t * rows : (t + 1) * rows]
                piece = piece * cosines[...] + pltpu.roll(piece, HD // 2, 1) * sines[...]
                lanes = (j * PACK + t) * HD
                dqs[c, :, lanes : lanes + HD] = piece.astype(BF16)
        for target in range(rank):
            part = slice(target * rows, (target + 1) * rows)
            staged[c, target, :, 0:HD] = key_sum[part].astype(BF16)
            staged[c, target, :, HD : 2 * HD] = value_sum[part].astype(BF16)
            back(c, rank, target).start()
        own[c, :, 0:HD] = key_sum[span - rows :]
        own[c, :, HD : 2 * HD] = value_sum[span - rows :]
        up_class[c] = adapter_scale * dot(low_of(0), dqs[c], 1, 0)
        mixed_q[...] += dot(dqs[c], up_heads[head].astype(BF16), 1, 1)

    def finish(c, rank):
        total = own[c]
        for sender in range(rank + 1, GROUP_DEV):
            back(c, sender, rank).wait_recv()
            total = total + returned[c, sender - 1].astype(F32)
        keys = total[:, 0:HD]
        keys = keys * cosines[...] + pltpu.roll(keys, HD // 2, 1) * sines[...]
        dkv[c, :, 0:HD] = keys.astype(BF16)
        dkv[c, :, HD : 2 * HD] = total[:, HD : 2 * HD].astype(BF16)

    def phase(low, high):
        early = HALF if low == 0 else 2

        def step(t):
            is_high = jnp.logical_and(t >= early, t < early + HALF)
            pl.when(is_high)(lambda: work(high_base + t - early, high))
            pl.when(jnp.logical_not(is_high))(
                lambda: work(low_base + jnp.where(t < early, t, t - HALF), low)
            )

        each_head(step, 0, KVH)

    pl.when(odd == 0)(lambda: phase(0, 2))
    pl.when(odd == 1)(lambda: phase(1, 3))

    position = positions_of(flags)
    for h in range(KVH):
        grad_proj[:, h * width : (h + 1) * width] = dqs[position[h]]
        up[:, h * width : (h + 1) * width] = up_class[position[h]]

    def collect(low, high):
        def last(i):
            finish(high_base + i, high)
            finish(low_base + i, low)

        each_head(last)

    pl.when(odd == 0)(lambda: collect(0, 2))
    pl.when(odd == 1)(lambda: collect(1, 3))

    for h in range(KVH):
        kvn[:, h * HD : (h + 1) * HD] = dkv[position[h], :, 0:HD]
        kvn[:, width_kv + h * HD : width_kv + (h + 1) * HD] = dkv[position[h], :, HD : 2 * HD]
    grad_proj[:, width_q : width_q + 2 * width_kv] = kvn[...]
    up[:, width_q : width_q + width_kv] = adapter_scale * dot(low_of(1), kvn[:, 0:width_kv], 1, 0)
    up[:, width_q + width_kv :] = adapter_scale * dot(low_of(2), kvn[:, width_kv:], 1, 0)
    mixed_k = dot(kvn[:, 0:width_kv], up_w[:, width_q : width_q + width_kv], 1, 1)
    mixed_v = dot(kvn[:, width_kv:], up_w[:, width_q + width_kv :], 1, 1)
    mixed = jnp.transpose(jnp.concatenate([mixed_q[...], mixed_k, mixed_v], axis=1)).astype(BF16)
    down_width = xv.shape[1] // SHARDS
    up_width = up.shape[1] // SHARDS
    zeros = jnp.zeros((8, HD), F32)
    for shard in range(SHARDS):
        down = adapter_scale * dot(mixed, xv[:, shard * down_width : (shard + 1) * down_width], 1, 0)
        mine = up[:, shard * up_width : (shard + 1) * up_width]
        rest = jnp.concatenate(
            [mine[:, 2 * HD :], jnp.zeros((8, 3 * HD - up_width), F32)], axis=1
        )
        at = packed_place(shard)
        packed[0, at] = jnp.concatenate([down[:, 0:HD], mine[:, 0:HD], rest, zeros], 0).astype(BF16)
        packed[1, at] = jnp.concatenate(
            [down[:, HD:], mine[:, HD : 2 * HD], zeros, zeros], 0
        ).astype(BF16)

    def remote(src, dst, send, recv, target):
        return pltpu.make_async_remote_copy(
            src_ref=src,
            dst_ref=dst,
            send_sem=send,
            recv_sem=recv,
            device_id=target,
            device_id_type=MESH,
        )

    first = remote(packed.at[1 - core], got1, send1, recv1, mate)
    first.start()
    first.wait_recv()

    def both(t):
        part = pl.ds(2 * t, 2)
        return packed[core, part].astype(F32) + got1[part].astype(F32)

    def second(k):
        t = in_plane(k)
        part = pl.ds(2 * t, 2)
        return remote(
            sum1.at[part], got2.at[plane], send2.at[k], recv2.at[plane], device(t, y, core)
        )

    def send_second(k, _):
        t = in_plane(k)
        sum1[pl.ds(2 * t, 2)] = both(t).astype(BF16)
        second(k).start()
        return 0

    lax.fori_loop(1, PLANE, send_second, 0)
    total = both(plane)

    def add_second(k, total):
        source = in_plane(PLANE - k)
        remote(
            sum1.at[pl.ds(0, 2)], got2.at[source], send2.at[k], recv2.at[source], mate
        ).wait_recv()
        return total + got2[source].astype(F32)

    sum2[...] = lax.fori_loop(1, PLANE, add_second, total)

    def third(step):
        target = in_ring(step)
        return remote(
            sum2.at[lax.div(target, 2)],
            got3.at[y],
            send3.at[step],
            recv3.at[y],
            device(plane, target, core),
        )

    for step in range(1, RING):
        third(step).start()
    got3[y] = sum2[y_high]
    for step in range(1, RING):
        source = in_ring(step)
        remote(sum2.at[0], got3.at[source], send3.at[step], recv3.at[source], mate).wait_recv()
    mine = got3[0] + got3[1] + got3[2] + got3[3]
    halves[core] = mine
    fourth = remote(halves.at[core], halves.at[core], send4, recv4, mate)
    fourth.start()
    squares = mine * mine
    norms[plane] = functools.reduce(
        lambda a, b: a + b, [squares[8 * r : 8 * (r + 1)] for r in range(PIECE // 8)]
    )

    def fifth(k):
        return remote(
            norms.at[plane], norms.at[plane], send5.at[k], recv5.at[plane], device(in_plane(k), y, core)
        )

    def fifth_arrival(k):
        source = in_plane(k)
        return remote(norms.at[source], norms.at[source], send5.at[k], recv5.at[source], mate)

    lax.fori_loop(1, PLANE, lambda k, _: (fifth(k).start(), 0)[1], 0)
    lax.fori_loop(1, PLANE, lambda k, _: (fifth_arrival(k).wait_recv(), 0)[1], 0)
    code = core * 2 + y_high
    quarters[code] = jnp.sum(norms[...], axis=0)

    def sixth(step):
        return remote(
            quarters.at[code], quarters.at[code], send6.at[step], recv6.at[code], quarter_device(step)
        )

    for step in range(1, 4):
        sixth(step).start()
    remote(halves.at[core], halves.at[1 - core], send4, recv4, mate).wait_recv()
    down_out[:, 0:HD] = halves[0, 0:24]
    down_out[:, HD : 2 * HD] = halves[1, 0:24]
    up_out[:, 0:HD] = halves[0, 24:32]
    up_out[:, HD : 2 * HD] = halves[1, 24:32]
    up_out[:, 2 * HD :] = halves[0, 32:40, 0 : up_out.shape[1] - 2 * HD]
    for step in range(1, 4):
        source = lax.rem(code + step, 4)
        remote(
            quarters.at[source], quarters.at[source], send6.at[step], recv6.at[source], mate
        ).wait_recv()
    everything = jnp.sum(jnp.sum(quarters[...], axis=0), keepdims=True)
    norm_out[...] = jnp.broadcast_to(jnp.sqrt(everything), norm_out.shape)

    first.wait_send()
    fourth.wait_send()
    lax.fori_loop(1, PLANE, lambda k, _: (second(k).wait_send(), 0)[1], 0)
    lax.fori_loop(1, PLANE, lambda k, _: (fifth(k).wait_send(), 0)[1], 0)
    for step in range(1, 4):
        third(step).wait_send()
        sixth(step).wait_send()

    def drain(low, high):
        def wait(i):
            for base, rank in ((low_base, low), (high_base, high)):
                for distance in range(1, GROUP_DEV - rank):
                    forward(base + i, rank, distance).wait_send()
                for target in range(rank):
                    back(base + i, rank, target).wait_send()

        each_head(wait)

    pl.when(odd == 0)(lambda: drain(0, 2))
    pl.when(odd == 1)(lambda: drain(1, 3))


def rotary_constants(rows, blocks):
    freqs = rope_base ** (-2.0 * np.arange(HD // 2) / HD)

    def table(positions, scale):
        angles = positions[:, None] * freqs[None, :]
        cosines, sines = np.cos(angles), np.sin(angles)
        both = np.stack(
            [np.concatenate([cosines, cosines], 1), np.concatenate([sines, -sines], 1)]
        )
        return jnp.asarray((both * scale).astype(np.float32))

    return table(np.arange(rows), 1.0), table(np.arange(blocks) * rows, SCALE)


def local(
    normed_layer_input,
    query,
    saved_key_value,
    output_gradient,
    adapter_down_weight,
    adapter_up_weight,
    shifted_head_flags,
):
    rows, model = normed_layer_input.shape[1:]
    columns = adapter_up_weight.shape[1]
    width = GROUP_HEADS * HD
    row_table, block_table = rotary_constants(rows, lax.axis_size("ctx"))
    dma = pltpu.SemaphoreType.DMA
    grad_proj, grad_down, grad_up, norm = pl.pallas_call(
        kernel,
        out_shape=(
            jax.ShapeDtypeStruct((rows, columns), BF16),
            jax.ShapeDtypeStruct((3 * ADAPTER_RANK, model // SHARDS), F32),
            jax.ShapeDtypeStruct((ADAPTER_RANK, columns // SHARDS), F32),
            jax.ShapeDtypeStruct((8, HD), F32),
        ),
        in_specs=[SMEM, HBM, HBM, HBM, HBM, VMEM, VMEM, VMEM, VMEM],
        out_specs=(VMEM, VMEM, VMEM, VMEM),
        scratch_shapes=[
            pltpu.VMEM((rows, model), BF16),
            pltpu.VMEM((2 * KVH, rows, HD), BF16),
            pltpu.VMEM((KVH, rows, width), BF16),
            pltpu.VMEM((KVH, rows, width), BF16),
            pltpu.VMEM((KVH, GROUP_DEV * rows, 2 * HD), BF16),
            pltpu.VMEM((KVH, GROUP_DEV - 1, rows, 2 * HD), BF16),
            pltpu.VMEM((KVH, GROUP_DEV - 1, rows, 2 * HD), BF16),
            pltpu.VMEM((KVH, rows, 2 * HD), F32),
            pltpu.VMEM((KVH, rows, width), BF16),
            pltpu.VMEM((KVH, rows, 2 * HD), BF16),
            pltpu.VMEM((rows, 2 * KVH * HD), BF16),
            pltpu.VMEM((rows, HD), F32),
            pltpu.VMEM((rows, HD), F32),
            pltpu.VMEM((3 * ADAPTER_RANK, rows), F32),
            pltpu.VMEM((KVH, ADAPTER_RANK, width), F32),
            pltpu.VMEM((ADAPTER_RANK, columns), F32),
            pltpu.VMEM((KVH, ADAPTER_RANK, width), F32),
            pltpu.VMEM((rows, ADAPTER_RANK), F32),
            pltpu.VMEM((2, SHARDS, PIECE, HD), BF16),
            pltpu.VMEM((SHARDS, PIECE, HD), BF16),
            pltpu.VMEM((SHARDS, PIECE, HD), BF16),
            pltpu.VMEM((PLANE, 2, PIECE, HD), BF16),
            pltpu.VMEM((2, PIECE, HD), F32),
            pltpu.VMEM((RING, PIECE, HD), F32),
            pltpu.VMEM((2, PIECE, HD), F32),
            pltpu.VMEM((PLANE, 8, HD), F32),
            pltpu.VMEM((4, 8, HD), F32),
            dma,
            dma((2 * KVH,)),
            dma((2, KVH)),
            dma((KVH, GROUP_DEV - 1)),
            dma((KVH, GROUP_DEV - 1)),
            dma((KVH, GROUP_DEV - 1)),
            dma((KVH, GROUP_DEV - 1)),
            dma,
            dma,
            dma((PLANE,)),
            dma((PLANE,)),
            dma((RING,)),
            dma((RING,)),
            dma,
            dma,
            dma((PLANE,)),
            dma((PLANE,)),
            dma((4,)),
            dma((4,)),
        ],
        compiler_params=pltpu.CompilerParams(
            collective_id=0, has_side_effects=True, vmem_limit_bytes=36 * 2**20
        ),
        name="attention_and_adapter_gradients",
    )(
        shifted_head_flags,
        normed_layer_input[0],
        query[0],
        saved_key_value[0],
        output_gradient[0],
        adapter_down_weight,
        adapter_up_weight,
        row_table,
        block_table,
    )
    return (grad_proj[None], grad_down, grad_up, norm[0, 0])


def solution(mesh):
    return jax.shard_map(
        local,
        mesh=mesh,
        in_specs=(
            P("dp", "ctx", None),
            P("dp", "ctx", None),
            P("dp", "ctx", None),
            P("dp", "ctx", None),
            P(),
            P(),
            P(),
        ),
        out_specs=(P("dp", "ctx", None), P(None, "ctx"), P(None, "ctx"), P()),
        check_vma=False,
    )
```

```python
import functools
import math

import jax
import jax.numpy as jnp
import numpy as np
from jax import lax
from jax.experimental import pallas as pl
from jax.experimental.pallas import tpu as pltpu
from jax.sharding import PartitionSpec as P

HQ = 64
KVH = 8
HD = 128
HALF = KVH // 2
GROUP_HEADS = HQ // KVH
ADAPTER_RANK = 8
GROUP_DEV = 4
PACK = 4
SHARDS = 32
PIECE = 48
RING = 4
PLANE = 16

rope_base = 10000.0
adapter_scale = 2.0
SCALE = HD ** (-0.5)
SCALE_LOG2 = SCALE * math.log2(math.e)
MESH = pl.DeviceIdType.MESH
VMEM = pl.BlockSpec(memory_space=pltpu.VMEM)
SMEM = pl.BlockSpec(memory_space=pltpu.SMEM)
HBM = pl.BlockSpec(memory_space=pltpu.HBM)
F32 = jnp.float32
BF16 = jnp.bfloat16


def head_at(flags, position):
    ones = jnp.int32(0)
    head = jnp.int32(0)
    for h in range(KVH):
        flag = jnp.minimum(flags[h], 1)
        here = (1 - flag) * (h - ones) + flag * (HALF + ones)
        head = head + h * (here == position).astype(jnp.int32)
        ones = ones + flag
    return head


def positions_of(flags):
    ones = jnp.int32(0)
    found = []
    for h in range(KVH):
        flag = jnp.minimum(flags[h], 1)
        found.append((1 - flag) * (h - ones) + flag * (HALF + ones))
        ones = ones + flag
    return found


def dot(a, b, ca, cb):
    return lax.dot_general(a, b, (((ca,), (cb,)), ((), ())), preferred_element_type=F32)


def packed_place(shard):
    z, rest = divmod(shard, 8)
    high, x = divmod(rest, 4)
    return (z * 4 + x) * 2 + high


def kernel(
    flags,
    x_hbm,
    q_hbm,
    kv_hbm,
    g_hbm,
    down_hbm,
    up_hbm,
    row_hbm,
    block_hbm,
    grad_proj,
    down_out,
    up_out,
    norm_out,
    xv,
    kv_rows,
    kv,
    down_w,
    up_w,
    row_table,
    block_table,
    qv,
    gv,
    window,
    staged,
    returned,
    own,
    dqs,
    dkv,
    kvn,
    cosines,
    sines,
    low_t,
    up_heads,
    up,
    up_class,
    mixed_q,
    packed,
    got1,
    sum1,
    got2,
    sum2,
    got3,
    halves,
    norms,
    quarters,
    small_sem,
    x_sem,
    kv_sem,
    in_sem,
    fsend,
    frecv,
    bsend,
    brecv,
    send1,
    recv1,
    send2,
    recv2,
    send3,
    recv3,
    send4,
    recv4,
    send5,
    recv5,
    send6,
    recv6,
):
    rows = q_hbm.shape[0]
    dp = lax.axis_index("dp")
    place = lax.axis_index("ctx")
    count = lax.axis_size("ctx")
    odd = lax.rem(place, 2)
    first_rank = lax.rem(place, GROUP_DEV)
    second_rank = lax.rem(place + 2, GROUP_DEV)
    low_base = jnp.where(first_rank < 2, 0, HALF)
    high_base = HALF - low_base
    core = lax.rem(dp, 2)
    y_low = lax.div(dp, 2)
    y_high = lax.rem(lax.div(place, 4), 2)
    y = y_high * 2 + y_low
    plane = lax.div(place, 8) * 4 + lax.rem(place, 4)
    width = GROUP_HEADS * HD
    width_q = HQ * HD
    width_kv = KVH * HD
    rank_a = ADAPTER_RANK

    kv_in = pltpu.make_async_copy(kv_hbm, kv_rows, kv_sem)
    kv_in.start()

    def peer(offset):
        return (dp, lax.rem(place + offset + count, count))

    def device(plane, y, core):
        high, low = lax.div(y, 2), lax.rem(y, 2)
        return (low * 2 + core, lax.div(plane, 4) * 8 + high * 4 + lax.rem(plane, 4))

    def in_plane(step):
        return lax.rem(plane + step, PLANE)

    def in_ring(step):
        return lax.rem(y + step, RING)

    def quarter_device(step):
        code = lax.rem(core * 2 + y_high + step, 4)
        return device(plane, lax.rem(code, 2) * 2 + y_low, lax.div(code, 2))

    mate = device(plane, y, 1 - core)
    barrier = pltpu.get_barrier_semaphore()

    def greet(target):
        pl.semaphore_signal(barrier, inc=1, device_id=target, device_id_type=MESH)

    for rank in (first_rank, second_rank):
        for step in range(1, GROUP_DEV):
            greet(peer(lax.rem(rank + step, GROUP_DEV) - rank))
    lax.fori_loop(1, PLANE, lambda k, _: (greet(device(in_plane(k), y, core)), 0)[1], 0)
    for step in range(1, RING):
        greet(device(plane, in_ring(step), core))
        greet(quarter_device(step))
    greet(mate)

    copies_in = []
    for h in range(KVH):
        part = slice(h * width, (h + 1) * width)
        copies_in.append(pltpu.make_async_copy(q_hbm.at[:, part], qv.at[h], in_sem.at[0, h]))
        copies_in.append(pltpu.make_async_copy(g_hbm.at[:, part], gv.at[h], in_sem.at[1, h]))
    small_in = [
        pltpu.make_async_copy(source, target, small_sem.at[i])
        for i, (source, target) in enumerate(
            [(row_hbm, row_table), (block_hbm, block_table), (up_hbm, up_w), (down_hbm, down_w)]
        )
    ]
    x_in = pltpu.make_async_copy(x_hbm, xv, x_sem)
    kv_in.wait()
    for copy in copies_in + small_in + [x_in]:
        copy.start()
    for h in range(2 * KVH):
        kv[h] = kv_rows[:, h * HD : (h + 1) * HD]
    for c in range(KVH):
        rank = first_rank if c < HALF else second_rank
        head = head_at(flags, c)
        slot = pl.ds(pl.multiple_of(rank * rows, rows), rows)
        window[c, slot, 0:HD] = kv[head]
        window[c, slot, HD : 2 * HD] = kv[head + KVH]

    pl.semaphore_wait(barrier, 2 * (GROUP_DEV - 1) + PLANE - 1 + 2 * (RING - 1) + 1)

    def forward(c, rank, distance):
        part = window.at[c, rank * rows : (rank + 1) * rows]
        return pltpu.make_async_remote_copy(
            src_ref=part,
            dst_ref=part,
            send_sem=fsend.at[c, distance - 1],
            recv_sem=frecv.at[c, rank],
            device_id=peer(distance),
            device_id_type=MESH,
        )

    def back(c, rank, target):
        return pltpu.make_async_remote_copy(
            src_ref=staged.at[c, target],
            dst_ref=returned.at[c, rank - 1],
            send_sem=bsend.at[c, target],
            recv_sem=brecv.at[c, rank - 1],
            device_id=peer(target - rank),
            device_id_type=MESH,
        )

    def each_head(step, start=0, stop=HALF):
        lax.fori_loop(start, stop, lambda i, _: (step(i), 0)[1], 0)

    def sends(low, high):
        if low == 0:
            each_head(lambda i: forward(low_base + i, 0, 1).start(), 0, 2)

        def send_all(i):
            for base, rank in ((low_base, low), (high_base, high)):
                for distance in range(2 if rank == 0 else 1, GROUP_DEV - rank):
                    forward(base + i, rank, distance).start()

        each_head(send_all)
        if low == 0:
            each_head(lambda i: forward(low_base + i, 0, 1).start(), 2, HALF)

    pl.when(odd == 0)(lambda: sends(0, 2))
    pl.when(odd == 1)(lambda: sends(1, 3))

    for copy in small_in:
        copy.wait()
    block_cos, block_sin = block_table[0, pl.ds(place, 1)], block_table[1, pl.ds(place, 1)]
    row_cos, row_sin = row_table[0], row_table[1]
    cosines[...] = block_cos * row_cos - block_sin * row_sin
    sines[...] = block_sin * row_cos + block_cos * row_sin
    for h in range(KVH):
        up_heads[h] = up_w[:, h * width : (h + 1) * width].astype(F32)
    mixed_q[...] = jnp.zeros_like(mixed_q)
    for copy in copies_in:
        copy.wait()
    x_in.wait()
    low_t[...] = jnp.transpose(dot(xv[...], down_w[...], 1, 1))

    def low_of(segment):
        return low_t[segment * rank_a : (segment + 1) * rank_a].astype(BF16)

    def work(c, rank):
        blocks = rank + 1
        span = blocks * rows
        for source in range(rank):
            forward(c, source, rank - source).wait_recv()
        head = head_at(flags, c)
        keys = window[c, 0:span, 0:HD]
        values = window[c, 0:span, HD : 2 * HD]
        packed_rows = PACK * rows
        row = lax.broadcasted_iota(jnp.int32, (rows, packed_rows), 0)
        column = lax.rem(lax.broadcasted_iota(jnp.int32, (rows, packed_rows), 1), rows)
        allowed = row <= column
        key_sum, value_sum = None, None
        for j in range(GROUP_HEADS // PACK):

            def stacked(ref):
                return jnp.concatenate(
                    [ref[head, :, (j * PACK + t) * HD : (j * PACK + t + 1) * HD] for t in range(PACK)],
                    axis=0,
                )

            queries = stacked(qv)
            grads = stacked(gv)
            scores = dot(keys, queries, 1, 1)
            grad_probs = dot(values, grads, 1, 1)
            last = jnp.where(allowed, scores[span - rows :], -1e30)
            scores = jnp.concatenate([scores[: span - rows], last], axis=0) if rank else last
            peak = jnp.max(scores, axis=0, keepdims=True)
            weights = jnp.exp2((scores - peak) * SCALE_LOG2)
            probs = weights * (1.0 / jnp.sum(weights, axis=0, keepdims=True))
            inner = jnp.sum(probs * grad_probs, axis=0, keepdims=True)
            probs_low = probs.astype(BF16)
            grad_scores = (probs * (grad_probs - inner)).astype(BF16)
            value_term = dot(probs_low, grads, 1, 0)
            key_term = dot(grad_scores, queries, 1, 0)
            value_sum = value_term if value_sum is None else value_sum + value_term
            key_sum = key_term if key_sum is None else key_sum + key_term
            grad_query = dot(grad_scores, keys, 0, 0)
            for t in range(PACK):
                piece = grad_query[t * rows : (t + 1) * rows]
                piece = piece * cosines[...] + pltpu.roll(piece, HD // 2, 1) * sines[...]
                lanes = (j * PACK + t) * HD
                dqs[c, :, lanes : lanes + HD] = piece.astype(BF16)
        for target in range(rank):
            part = slice(target * rows, (target + 1) * rows)
            staged[c, target, :, 0:HD] = key_sum[part].astype(BF16)
            staged[c, target, :, HD : 2 * HD] = value_sum[part].astype(BF16)
            back(c, rank, target).start()
        own[c, :, 0:HD] = key_sum[span - rows :]
        own[c, :, HD : 2 * HD] = value_sum[span - rows :]
        up_class[c] = adapter_scale * dot(low_of(0), dqs[c], 1, 0)
        mixed_q[...] += dot(dqs[c], up_heads[head].astype(BF16), 1, 1)

    def finish(c, rank):
        total = own[c]
        for sender in range(rank + 1, GROUP_DEV):
            back(c, sender, rank).wait_recv()
            total = total + returned[c, sender - 1].astype(F32)
        keys = total[:, 0:HD]
        keys = keys * cosines[...] + pltpu.roll(keys, HD // 2, 1) * sines[...]
        dkv[c, :, 0:HD] = keys.astype(BF16)
        dkv[c, :, HD : 2 * HD] = total[:, HD : 2 * HD].astype(BF16)

    def phase(low, high):
        early = HALF if low == 0 else 2

        def step(t):
            is_high = jnp.logical_and(t >= early, t < early + HALF)
            pl.when(is_high)(lambda: work(high_base + t - early, high))
            pl.when(jnp.logical_not(is_high))(
                lambda: work(low_base + jnp.where(t < early, t, t - HALF), low)
            )

        each_head(step, 0, KVH)

    pl.when(odd == 0)(lambda: phase(0, 2))
    pl.when(odd == 1)(lambda: phase(1, 3))

    position = positions_of(flags)
    for h in range(KVH):
        grad_proj[:, h * width : (h + 1) * width] = dqs[position[h]]
        up[:, h * width : (h + 1) * width] = up_class[position[h]]

    def collect(low, high):
        def last(i):
            finish(high_base + i, high)
            finish(low_base + i, low)

        each_head(last)

    pl.when(odd == 0)(lambda: collect(0, 2))
    pl.when(odd == 1)(lambda: collect(1, 3))

    for h in range(KVH):
        kvn[:, h * HD : (h + 1) * HD] = dkv[position[h], :, 0:HD]
        kvn[:, width_kv + h * HD : width_kv + (h + 1) * HD] = dkv[position[h], :, HD : 2 * HD]
    grad_proj[:, width_q : width_q + 2 * width_kv] = kvn[...]
    up[:, width_q : width_q + width_kv] = adapter_scale * dot(low_of(1), kvn[:, 0:width_kv], 1, 0)
    up[:, width_q + width_kv :] = adapter_scale * dot(low_of(2), kvn[:, width_kv:], 1, 0)
    mixed_k = dot(kvn[:, 0:width_kv], up_w[:, width_q : width_q + width_kv], 1, 1)
    mixed_v = dot(kvn[:, width_kv:], up_w[:, width_q + width_kv :], 1, 1)
    mixed = jnp.transpose(jnp.concatenate([mixed_q[...], mixed_k, mixed_v], axis=1)).astype(BF16)
    down_width = xv.shape[1] // SHARDS
    up_width = up.shape[1] // SHARDS
    zeros = jnp.zeros((8, HD), F32)
    for shard in range(SHARDS):
        down = adapter_scale * dot(mixed, xv[:, shard * down_width : (shard + 1) * down_width], 1, 0)
        mine = up[:, shard * up_width : (shard + 1) * up_width]
        rest = jnp.concatenate(
            [mine[:, 2 * HD :], jnp.zeros((8, 3 * HD - up_width), F32)], axis=1
        )
        at = packed_place(shard)
        packed[0, at] = jnp.concatenate([down[:, 0:HD], mine[:, 0:HD], rest, zeros], 0).astype(BF16)
        packed[1, at] = jnp.concatenate(
            [down[:, HD:], mine[:, HD : 2 * HD], zeros, zeros], 0
        ).astype(BF16)

    def remote(src, dst, send, recv, target):
        return pltpu.make_async_remote_copy(
            src_ref=src,
            dst_ref=dst,
            send_sem=send,
            recv_sem=recv,
            device_id=target,
            device_id_type=MESH,
        )

    first = remote(packed.at[1 - core], got1, send1, recv1, mate)
    first.start()
    first.wait_recv()

    def both(t):
        part = pl.ds(2 * t, 2)
        return packed[core, part].astype(F32) + got1[part].astype(F32)

    def second(k):
        t = in_plane(k)
        part = pl.ds(2 * t, 2)
        return remote(
            sum1.at[part], got2.at[plane], send2.at[k], recv2.at[plane], device(t, y, core)
        )

    def send_second(k, _):
        t = in_plane(k)
        sum1[pl.ds(2 * t, 2)] = both(t).astype(BF16)
        second(k).start()
        return 0

    lax.fori_loop(1, PLANE, send_second, 0)
    total = both(plane)

    def add_second(k, total):
        source = in_plane(PLANE - k)
        remote(
            sum1.at[pl.ds(0, 2)], got2.at[source], send2.at[k], recv2.at[source], mate
        ).wait_recv()
        return total + got2[source].astype(F32)

    sum2[...] = lax.fori_loop(1, PLANE, add_second, total)

    def third(step):
        target = in_ring(step)
        return remote(
            sum2.at[lax.div(target, 2)],
            got3.at[y],
            send3.at[step],
            recv3.at[y],
            device(plane, target, core),
        )

    for step in range(1, RING):
        third(step).start()
    got3[y] = sum2[y_high]
    for step in range(1, RING):
        source = in_ring(step)
        remote(sum2.at[0], got3.at[source], send3.at[step], recv3.at[source], mate).wait_recv()
    mine = got3[0] + got3[1] + got3[2] + got3[3]
    halves[core] = mine
    fourth = remote(halves.at[core], halves.at[core], send4, recv4, mate)
    fourth.start()
    squares = mine * mine
    norms[plane] = functools.reduce(
        lambda a, b: a + b, [squares[8 * r : 8 * (r + 1)] for r in range(PIECE // 8)]
    )

    def fifth(k):
        return remote(
            norms.at[plane], norms.at[plane], send5.at[k], recv5.at[plane], device(in_plane(k), y, core)
        )

    def fifth_arrival(k):
        source = in_plane(k)
        return remote(norms.at[source], norms.at[source], send5.at[k], recv5.at[source], mate)

    lax.fori_loop(1, PLANE, lambda k, _: (fifth(k).start(), 0)[1], 0)
    lax.fori_loop(1, PLANE, lambda k, _: (fifth_arrival(k).wait_recv(), 0)[1], 0)
    code = core * 2 + y_high
    quarters[code] = jnp.sum(norms[...], axis=0)

    def sixth(step):
        return remote(
            quarters.at[code], quarters.at[code], send6.at[step], recv6.at[code], quarter_device(step)
        )

    for step in range(1, 4):
        sixth(step).start()
    remote(halves.at[core], halves.at[1 - core], send4, recv4, mate).wait_recv()
    down_out[:, 0:HD] = halves[0, 0:24]
    down_out[:, HD : 2 * HD] = halves[1, 0:24]
    up_out[:, 0:HD] = halves[0, 24:32]
    up_out[:, HD : 2 * HD] = halves[1, 24:32]
    up_out[:, 2 * HD :] = halves[0, 32:40, 0 : up_out.shape[1] - 2 * HD]
    for step in range(1, 4):
        source = lax.rem(code + step, 4)
        remote(
            quarters.at[source], quarters.at[source], send6.at[step], recv6.at[source], mate
        ).wait_recv()
    everything = jnp.sum(jnp.sum(quarters[...], axis=0), keepdims=True)
    norm_out[...] = jnp.broadcast_to(jnp.sqrt(everything), norm_out.shape)

    first.wait_send()
    fourth.wait_send()
    lax.fori_loop(1, PLANE, lambda k, _: (second(k).wait_send(), 0)[1], 0)
    lax.fori_loop(1, PLANE, lambda k, _: (fifth(k).wait_send(), 0)[1], 0)
    for step in range(1, 4):
        third(step).wait_send()
        sixth(step).wait_send()

    def drain(low, high):
        def wait(i):
            for base, rank in ((low_base, low), (high_base, high)):
                for distance in range(1, GROUP_DEV - rank):
                    forward(base + i, rank, distance).wait_send()
                for target in range(rank):
                    back(base + i, rank, target).wait_send()

        each_head(wait)

    pl.when(odd == 0)(lambda: drain(0, 2))
    pl.when(odd == 1)(lambda: drain(1, 3))


def rotary_constants(rows, blocks):
    freqs = rope_base ** (-2.0 * np.arange(HD // 2) / HD)

    def table(positions, scale):
        angles = positions[:, None] * freqs[None, :]
        cosines, sines = np.cos(angles), np.sin(angles)
        both = np.stack(
            [np.concatenate([cosines, cosines], 1), np.concatenate([sines, -sines], 1)]
        )
        return jnp.asarray((both * scale).astype(np.float32))

    return table(np.arange(rows), 1.0), table(np.arange(blocks) * rows, SCALE)


def local(
    normed_layer_input,
    query,
    saved_key_value,
    output_gradient,
    adapter_down_weight,
    adapter_up_weight,
    shifted_head_flags,
):
    rows, model = normed_layer_input.shape[1:]
    columns = adapter_up_weight.shape[1]
    width = GROUP_HEADS * HD
    row_table, block_table = rotary_constants(rows, lax.axis_size("ctx"))
    dma = pltpu.SemaphoreType.DMA
    grad_proj, grad_down, grad_up, norm = pl.pallas_call(
        kernel,
        out_shape=(
            pltpu.VMEM((rows, columns), BF16),
            jax.ShapeDtypeStruct((3 * ADAPTER_RANK, model // SHARDS), F32),
            jax.ShapeDtypeStruct((ADAPTER_RANK, columns // SHARDS), F32),
            jax.ShapeDtypeStruct((8, HD), F32),
        ),
        in_specs=[SMEM] + [HBM] * 8,
        out_specs=(VMEM, VMEM, VMEM, VMEM),
        scratch_shapes=[
            pltpu.VMEM((rows, model), BF16),
            pltpu.VMEM((rows, 2 * KVH * HD), BF16),
            pltpu.VMEM((2 * KVH, rows, HD), BF16),
            pltpu.VMEM((3 * ADAPTER_RANK, model), BF16),
            pltpu.VMEM((ADAPTER_RANK, columns), BF16),
            pltpu.VMEM(row_table.shape, F32),
            pltpu.VMEM(block_table.shape, F32),
            pltpu.VMEM((KVH, rows, width), BF16),
            pltpu.VMEM((KVH, rows, width), BF16),
            pltpu.VMEM((KVH, GROUP_DEV * rows, 2 * HD), BF16),
            pltpu.VMEM((KVH, GROUP_DEV - 1, rows, 2 * HD), BF16),
            pltpu.VMEM((KVH, GROUP_DEV - 1, rows, 2 * HD), BF16),
            pltpu.VMEM((KVH, rows, 2 * HD), F32),
            pltpu.VMEM((KVH, rows, width), BF16),
            pltpu.VMEM((KVH, rows, 2 * HD), BF16),
            pltpu.VMEM((rows, 2 * KVH * HD), BF16),
            pltpu.VMEM((rows, HD), F32),
            pltpu.VMEM((rows, HD), F32),
            pltpu.VMEM((3 * ADAPTER_RANK, rows), F32),
            pltpu.VMEM((KVH, ADAPTER_RANK, width), F32),
            pltpu.VMEM((ADAPTER_RANK, columns), F32),
            pltpu.VMEM((KVH, ADAPTER_RANK, width), F32),
            pltpu.VMEM((rows, ADAPTER_RANK), F32),
            pltpu.VMEM((2, SHARDS, PIECE, HD), BF16),
            pltpu.VMEM((SHARDS, PIECE, HD), BF16),
            pltpu.VMEM((SHARDS, PIECE, HD), BF16),
            pltpu.VMEM((PLANE, 2, PIECE, HD), BF16),
            pltpu.VMEM((2, PIECE, HD), F32),
            pltpu.VMEM((RING, PIECE, HD), F32),
            pltpu.VMEM((2, PIECE, HD), F32),
            pltpu.VMEM((PLANE, 8, HD), F32),
            pltpu.VMEM((4, 8, HD), F32),
            dma((4,)),
            dma,
            dma,
            dma((2, KVH)),
            dma((KVH, GROUP_DEV - 1)),
            dma((KVH, GROUP_DEV - 1)),
            dma((KVH, GROUP_DEV - 1)),
            dma((KVH, GROUP_DEV - 1)),
            dma,
            dma,
            dma((PLANE,)),
            dma((PLANE,)),
            dma((RING,)),
            dma((RING,)),
            dma,
            dma,
            dma((PLANE,)),
            dma((PLANE,)),
            dma((4,)),
            dma((4,)),
        ],
        compiler_params=pltpu.CompilerParams(
            collective_id=0, has_side_effects=True, vmem_limit_bytes=48 * 2**20
        ),
        name="attention_and_adapter_gradients",
    )(
        shifted_head_flags,
        *(
            pltpu.with_memory_space_constraint(array, pltpu.HBM)
            for array in (
                normed_layer_input[0],
                query[0],
                saved_key_value[0],
                output_gradient[0],
                adapter_down_weight,
                adapter_up_weight,
                row_table,
                block_table,
            )
        ),
    )
    return (grad_proj[None], grad_down, grad_up, norm[0, 0])


def solution(mesh):
    return jax.shard_map(
        local,
        mesh=mesh,
        in_specs=(
            P("dp", "ctx", None),
            P("dp", "ctx", None),
            P("dp", "ctx", None),
            P("dp", "ctx", None),
            P(),
            P(),
            P(),
        ),
        out_specs=(P("dp", "ctx", None), P(None, "ctx"), P(None, "ctx"), P()),
        check_vma=False,
    )
```

```python
import functools
import math

import jax
import jax.numpy as jnp
import numpy as np
from jax import lax
from jax.experimental import pallas as pl
from jax.experimental.pallas import tpu as pltpu
from jax.sharding import PartitionSpec as P

HQ = 64
KVH = 8
HD = 128
HALF = KVH // 2
GROUP_HEADS = HQ // KVH
ADAPTER_RANK = 8
GROUP_DEV = 4
PACK = 4
SHARDS = 32
PIECE = 48
RING = 4
PLANE = 16

rope_base = 10000.0
adapter_scale = 2.0
SCALE = HD ** (-0.5)
SCALE_LOG2 = SCALE * math.log2(math.e)
MESH = pl.DeviceIdType.MESH
VMEM = pl.BlockSpec(memory_space=pltpu.VMEM)
SMEM = pl.BlockSpec(memory_space=pltpu.SMEM)
HBM = pl.BlockSpec(memory_space=pltpu.HBM)
F32 = jnp.float32
BF16 = jnp.bfloat16


def head_at(flags, position):
    ones = jnp.int32(0)
    head = jnp.int32(0)
    for h in range(KVH):
        flag = jnp.minimum(flags[h], 1)
        here = (1 - flag) * (h - ones) + flag * (HALF + ones)
        head = head + h * (here == position).astype(jnp.int32)
        ones = ones + flag
    return head


def positions_of(flags):
    ones = jnp.int32(0)
    found = []
    for h in range(KVH):
        flag = jnp.minimum(flags[h], 1)
        found.append((1 - flag) * (h - ones) + flag * (HALF + ones))
        ones = ones + flag
    return found


def dot(a, b, ca, cb):
    return lax.dot_general(a, b, (((ca,), (cb,)), ((), ())), preferred_element_type=F32)


def packed_place(shard):
    z, rest = divmod(shard, 8)
    high, x = divmod(rest, 4)
    return (z * 4 + x) * 2 + high


def kernel(
    flags,
    x_hbm,
    q_hbm,
    kv_hbm,
    g_hbm,
    down_hbm,
    up_hbm,
    row_hbm,
    block_hbm,
    grad_proj,
    down_out,
    up_out,
    norm_out,
    xv,
    kv_rows,
    kv,
    down_w,
    up_w,
    row_table,
    block_table,
    qv,
    gv,
    window,
    staged,
    returned,
    own,
    dqs,
    dkv,
    kvn,
    cosines,
    sines,
    low_t,
    up_heads,
    up,
    up_class,
    mixed_q,
    packed,
    got1,
    sum1,
    got2,
    sum2,
    got3,
    halves,
    norms,
    quarters,
    small_sem,
    x_sem,
    kv_sem,
    in_sem,
    fsend,
    frecv,
    bsend,
    brecv,
    send1,
    recv1,
    send2,
    recv2,
    send3,
    recv3,
    send4,
    recv4,
    send5,
    recv5,
    send6,
    recv6,
):
    rows = q_hbm.shape[0]
    dp = lax.axis_index("dp")
    place = lax.axis_index("ctx")
    count = lax.axis_size("ctx")
    odd = lax.rem(place, 2)
    first_rank = lax.rem(place, GROUP_DEV)
    second_rank = lax.rem(place + 2, GROUP_DEV)
    low_base = jnp.where(first_rank < 2, 0, HALF)
    high_base = HALF - low_base
    core = lax.rem(dp, 2)
    y_low = lax.div(dp, 2)
    y_high = lax.rem(lax.div(place, 4), 2)
    y = y_high * 2 + y_low
    plane = lax.div(place, 8) * 4 + lax.rem(place, 4)
    width = GROUP_HEADS * HD
    width_q = HQ * HD
    width_kv = KVH * HD
    rank_a = ADAPTER_RANK

    kv_in = pltpu.make_async_copy(kv_hbm, kv_rows, kv_sem)
    kv_in.start()

    def peer(offset):
        return (dp, lax.rem(place + offset + count, count))

    def device(plane, y, core):
        high, low = lax.div(y, 2), lax.rem(y, 2)
        return (low * 2 + core, lax.div(plane, 4) * 8 + high * 4 + lax.rem(plane, 4))

    def in_plane(step):
        return lax.rem(plane + step, PLANE)

    def in_ring(step):
        return lax.rem(y + step, RING)

    mate = device(plane, y, 1 - core)
    barrier = pltpu.get_barrier_semaphore()

    def greet(target):
        pl.semaphore_signal(barrier, inc=1, device_id=target, device_id_type=MESH)

    for rank in (first_rank, second_rank):
        for step in range(1, GROUP_DEV):
            greet(peer(lax.rem(rank + step, GROUP_DEV) - rank))
    lax.fori_loop(1, PLANE, lambda k, _: (greet(device(in_plane(k), y, core)), 0)[1], 0)
    for step in range(1, RING):
        greet(device(plane, in_ring(step), core))
    greet(mate)

    copies_in = []
    for h in range(KVH):
        part = slice(h * width, (h + 1) * width)
        copies_in.append(pltpu.make_async_copy(q_hbm.at[:, part], qv.at[h], in_sem.at[0, h]))
        copies_in.append(pltpu.make_async_copy(g_hbm.at[:, part], gv.at[h], in_sem.at[1, h]))
    small_in = [
        pltpu.make_async_copy(source, target, small_sem.at[i])
        for i, (source, target) in enumerate(
            [(row_hbm, row_table), (block_hbm, block_table), (up_hbm, up_w), (down_hbm, down_w)]
        )
    ]
    x_in = pltpu.make_async_copy(x_hbm, xv, x_sem)
    kv_in.wait()
    for copy in copies_in + small_in + [x_in]:
        copy.start()
    for h in range(2 * KVH):
        kv[h] = kv_rows[:, h * HD : (h + 1) * HD]
    for c in range(KVH):
        rank = first_rank if c < HALF else second_rank
        head = head_at(flags, c)
        slot = pl.ds(pl.multiple_of(rank * rows, rows), rows)
        window[c, slot, 0:HD] = kv[head]
        window[c, slot, HD : 2 * HD] = kv[head + KVH]

    pl.semaphore_wait(barrier, 2 * (GROUP_DEV - 1) + PLANE - 1 + RING - 1 + 1)

    def forward(c, rank, distance):
        part = window.at[c, rank * rows : (rank + 1) * rows]
        return pltpu.make_async_remote_copy(
            src_ref=part,
            dst_ref=part,
            send_sem=fsend.at[c, distance - 1],
            recv_sem=frecv.at[c, rank],
            device_id=peer(distance),
            device_id_type=MESH,
        )

    def back(c, rank, target):
        return pltpu.make_async_remote_copy(
            src_ref=staged.at[c, target],
            dst_ref=returned.at[c, rank - 1],
            send_sem=bsend.at[c, target],
            recv_sem=brecv.at[c, rank - 1],
            device_id=peer(target - rank),
            device_id_type=MESH,
        )

    def each_head(step, start=0, stop=HALF):
        lax.fori_loop(start, stop, lambda i, _: (step(i), 0)[1], 0)

    def sends(low, high):
        if low == 0:
            each_head(lambda i: forward(low_base + i, 0, 1).start(), 0, 2)

        def send_all(i):
            for base, rank in ((low_base, low), (high_base, high)):
                for distance in range(2 if rank == 0 else 1, GROUP_DEV - rank):
                    forward(base + i, rank, distance).start()

        each_head(send_all)
        if low == 0:
            each_head(lambda i: forward(low_base + i, 0, 1).start(), 2, HALF)

    pl.when(odd == 0)(lambda: sends(0, 2))
    pl.when(odd == 1)(lambda: sends(1, 3))

    for copy in small_in:
        copy.wait()
    block_cos, block_sin = block_table[0, pl.ds(place, 1)], block_table[1, pl.ds(place, 1)]
    row_cos, row_sin = row_table[0], row_table[1]
    cosines[...] = block_cos * row_cos - block_sin * row_sin
    sines[...] = block_sin * row_cos + block_cos * row_sin
    for h in range(KVH):
        up_heads[h] = up_w[:, h * width : (h + 1) * width].astype(F32)
    mixed_q[...] = jnp.zeros_like(mixed_q)
    for copy in copies_in:
        copy.wait()
    x_in.wait()
    low_t[...] = jnp.transpose(dot(xv[...], down_w[...], 1, 1))

    def low_of(segment):
        return low_t[segment * rank_a : (segment + 1) * rank_a].astype(BF16)

    def work(c, rank):
        blocks = rank + 1
        span = blocks * rows
        for source in range(rank):
            forward(c, source, rank - source).wait_recv()
        head = head_at(flags, c)
        keys = window[c, 0:span, 0:HD]
        values = window[c, 0:span, HD : 2 * HD]
        packed_rows = PACK * rows
        row = lax.broadcasted_iota(jnp.int32, (rows, packed_rows), 0)
        column = lax.rem(lax.broadcasted_iota(jnp.int32, (rows, packed_rows), 1), rows)
        allowed = row <= column
        key_sum, value_sum = None, None
        for j in range(GROUP_HEADS // PACK):

            def stacked(ref):
                return jnp.concatenate(
                    [ref[head, :, (j * PACK + t) * HD : (j * PACK + t + 1) * HD] for t in range(PACK)],
                    axis=0,
                )

            queries = stacked(qv)
            grads = stacked(gv)
            scores = dot(keys, queries, 1, 1)
            grad_probs = dot(values, grads, 1, 1)
            last = jnp.where(allowed, scores[span - rows :], -1e30)
            scores = jnp.concatenate([scores[: span - rows], last], axis=0) if rank else last
            peak = jnp.max(scores, axis=0, keepdims=True)
            weights = jnp.exp2((scores - peak) * SCALE_LOG2)
            probs = weights * (1.0 / jnp.sum(weights, axis=0, keepdims=True))
            inner = jnp.sum(probs * grad_probs, axis=0, keepdims=True)
            probs_low = probs.astype(BF16)
            grad_scores = (probs * (grad_probs - inner)).astype(BF16)
            value_term = dot(probs_low, grads, 1, 0)
            key_term = dot(grad_scores, queries, 1, 0)
            value_sum = value_term if value_sum is None else value_sum + value_term
            key_sum = key_term if key_sum is None else key_sum + key_term
            grad_query = dot(grad_scores, keys, 0, 0)
            for t in range(PACK):
                piece = grad_query[t * rows : (t + 1) * rows]
                piece = piece * cosines[...] + pltpu.roll(piece, HD // 2, 1) * sines[...]
                lanes = (j * PACK + t) * HD
                dqs[c, :, lanes : lanes + HD] = piece.astype(BF16)
        for target in range(rank):
            part = slice(target * rows, (target + 1) * rows)
            staged[c, target, :, 0:HD] = key_sum[part].astype(BF16)
            staged[c, target, :, HD : 2 * HD] = value_sum[part].astype(BF16)
            back(c, rank, target).start()
        own[c, :, 0:HD] = key_sum[span - rows :]
        own[c, :, HD : 2 * HD] = value_sum[span - rows :]
        up_class[c] = adapter_scale * dot(low_of(0), dqs[c], 1, 0)
        mixed_q[...] += dot(dqs[c], up_heads[head].astype(BF16), 1, 1)

    def finish(c, rank):
        total = own[c]
        for sender in range(rank + 1, GROUP_DEV):
            back(c, sender, rank).wait_recv()
            total = total + returned[c, sender - 1].astype(F32)
        keys = total[:, 0:HD]
        keys = keys * cosines[...] + pltpu.roll(keys, HD // 2, 1) * sines[...]
        dkv[c, :, 0:HD] = keys.astype(BF16)
        dkv[c, :, HD : 2 * HD] = total[:, HD : 2 * HD].astype(BF16)

    def phase(low, high):
        early = HALF if low == 0 else 2

        def step(t):
            is_high = jnp.logical_and(t >= early, t < early + HALF)
            pl.when(is_high)(lambda: work(high_base + t - early, high))
            pl.when(jnp.logical_not(is_high))(
                lambda: work(low_base + jnp.where(t < early, t, t - HALF), low)
            )

        each_head(step, 0, KVH)

    pl.when(odd == 0)(lambda: phase(0, 2))
    pl.when(odd == 1)(lambda: phase(1, 3))

    position = positions_of(flags)
    for h in range(KVH):
        grad_proj[:, h * width : (h + 1) * width] = dqs[position[h]]
        up[:, h * width : (h + 1) * width] = up_class[position[h]]

    def collect(low, high):
        def last(i):
            finish(high_base + i, high)
            finish(low_base + i, low)

        each_head(last)

    pl.when(odd == 0)(lambda: collect(0, 2))
    pl.when(odd == 1)(lambda: collect(1, 3))

    for h in range(KVH):
        kvn[:, h * HD : (h + 1) * HD] = dkv[position[h], :, 0:HD]
        kvn[:, width_kv + h * HD : width_kv + (h + 1) * HD] = dkv[position[h], :, HD : 2 * HD]
    grad_proj[:, width_q : width_q + 2 * width_kv] = kvn[...]
    up[:, width_q : width_q + width_kv] = adapter_scale * dot(low_of(1), kvn[:, 0:width_kv], 1, 0)
    up[:, width_q + width_kv :] = adapter_scale * dot(low_of(2), kvn[:, width_kv:], 1, 0)
    mixed_k = dot(kvn[:, 0:width_kv], up_w[:, width_q : width_q + width_kv], 1, 1)
    mixed_v = dot(kvn[:, width_kv:], up_w[:, width_q + width_kv :], 1, 1)
    mixed = jnp.transpose(jnp.concatenate([mixed_q[...], mixed_k, mixed_v], axis=1)).astype(BF16)
    down_width = xv.shape[1] // SHARDS
    up_width = up.shape[1] // SHARDS
    zeros = jnp.zeros((8, HD), F32)
    for shard in range(SHARDS):
        down = adapter_scale * dot(mixed, xv[:, shard * down_width : (shard + 1) * down_width], 1, 0)
        mine = up[:, shard * up_width : (shard + 1) * up_width]
        rest = jnp.concatenate(
            [mine[:, 2 * HD :], jnp.zeros((8, 3 * HD - up_width), F32)], axis=1
        )
        at = packed_place(shard)
        packed[0, at] = jnp.concatenate([down[:, 0:HD], mine[:, 0:HD], rest, zeros], 0).astype(BF16)
        packed[1, at] = jnp.concatenate(
            [down[:, HD:], mine[:, HD : 2 * HD], zeros, zeros], 0
        ).astype(BF16)

    def remote(src, dst, send, recv, target):
        return pltpu.make_async_remote_copy(
            src_ref=src,
            dst_ref=dst,
            send_sem=send,
            recv_sem=recv,
            device_id=target,
            device_id_type=MESH,
        )

    first = remote(packed.at[1 - core], got1, send1, recv1, mate)
    first.start()
    first.wait_recv()

    def both(t):
        part = pl.ds(2 * t, 2)
        return packed[core, part].astype(F32) + got1[part].astype(F32)

    def second(k):
        t = in_plane(k)
        part = pl.ds(2 * t, 2)
        return remote(
            sum1.at[part], got2.at[plane], send2.at[k], recv2.at[plane], device(t, y, core)
        )

    def send_second(k, _):
        t = in_plane(k)
        sum1[pl.ds(2 * t, 2)] = both(t).astype(BF16)
        second(k).start()
        return 0

    lax.fori_loop(1, PLANE, send_second, 0)
    total = both(plane)

    def add_second(k, total):
        source = in_plane(PLANE - k)
        remote(
            sum1.at[pl.ds(0, 2)], got2.at[source], send2.at[k], recv2.at[source], mate
        ).wait_recv()
        return total + got2[source].astype(F32)

    sum2[...] = lax.fori_loop(1, PLANE, add_second, total)

    got3[y] = sum2[...]

    def third(step):
        return remote(
            got3.at[y],
            got3.at[y],
            send3.at[step],
            recv3.at[y],
            device(plane, in_ring(step), core),
        )

    for step in range(1, RING):
        third(step).start()
    for step in range(1, RING):
        source = in_ring(step)
        remote(got3.at[source], got3.at[source], send3.at[step], recv3.at[source], mate).wait_recv()
    whole = got3[0] + got3[1] + got3[2] + got3[3]
    sum2[...] = whole
    halves[core] = sum2[y_high]
    fourth = remote(halves.at[core], halves.at[core], send4, recv4, mate)
    squares = whole * whole
    norms[plane] = functools.reduce(
        lambda a, b: a + b,
        [squares[h, 8 * r : 8 * (r + 1)] for h in range(2) for r in range(PIECE // 8)],
    )

    def fifth(k):
        return remote(
            norms.at[plane], norms.at[plane], send5.at[k], recv5.at[plane], device(in_plane(k), y, core)
        )

    def fifth_arrival(k):
        source = in_plane(k)
        return remote(norms.at[source], norms.at[source], send5.at[k], recv5.at[source], mate)

    lax.fori_loop(1, PLANE, lambda k, _: (fifth(k).start(), 0)[1], 0)
    fourth.start()
    remote(halves.at[core], halves.at[1 - core], send4, recv4, mate).wait_recv()
    down_out[:, 0:HD] = halves[0, 0:24]
    down_out[:, HD : 2 * HD] = halves[1, 0:24]
    up_out[:, 0:HD] = halves[0, 24:32]
    up_out[:, HD : 2 * HD] = halves[1, 24:32]
    up_out[:, 2 * HD :] = halves[0, 32:40, 0 : up_out.shape[1] - 2 * HD]
    lax.fori_loop(1, PLANE, lambda k, _: (fifth_arrival(k).wait_recv(), 0)[1], 0)
    quarters[core] = jnp.sum(norms[...], axis=0)
    sixth = remote(quarters.at[core], quarters.at[core], send6, recv6, mate)
    sixth.start()
    remote(quarters.at[1 - core], quarters.at[1 - core], send6, recv6, mate).wait_recv()
    everything = jnp.sum(quarters[0] + quarters[1], keepdims=True)
    norm_out[...] = jnp.sqrt(everything)

    first.wait_send()
    fourth.wait_send()
    lax.fori_loop(1, PLANE, lambda k, _: (second(k).wait_send(), 0)[1], 0)
    lax.fori_loop(1, PLANE, lambda k, _: (fifth(k).wait_send(), 0)[1], 0)
    for step in range(1, 4):
        third(step).wait_send()
    sixth.wait_send()

    def drain(low, high):
        def wait(i):
            for base, rank in ((low_base, low), (high_base, high)):
                for distance in range(1, GROUP_DEV - rank):
                    forward(base + i, rank, distance).wait_send()
                for target in range(rank):
                    back(base + i, rank, target).wait_send()

        each_head(wait)

    pl.when(odd == 0)(lambda: drain(0, 2))
    pl.when(odd == 1)(lambda: drain(1, 3))


def rotary_constants(rows, blocks):
    freqs = rope_base ** (-2.0 * np.arange(HD // 2) / HD)

    def table(positions, scale):
        angles = positions[:, None] * freqs[None, :]
        cosines, sines = np.cos(angles), np.sin(angles)
        both = np.stack(
            [np.concatenate([cosines, cosines], 1), np.concatenate([sines, -sines], 1)]
        )
        return jnp.asarray((both * scale).astype(np.float32))

    return table(np.arange(rows), 1.0), table(np.arange(blocks) * rows, SCALE)


def local(
    normed_layer_input,
    query,
    saved_key_value,
    output_gradient,
    adapter_down_weight,
    adapter_up_weight,
    shifted_head_flags,
):
    rows, model = normed_layer_input.shape[1:]
    columns = adapter_up_weight.shape[1]
    width = GROUP_HEADS * HD
    row_table, block_table = rotary_constants(rows, lax.axis_size("ctx"))
    dma = pltpu.SemaphoreType.DMA
    grad_proj, grad_down, grad_up, norm = pl.pallas_call(
        kernel,
        out_shape=(
            pltpu.VMEM((rows, columns), BF16),
            jax.ShapeDtypeStruct((3 * ADAPTER_RANK, model // SHARDS), F32),
            jax.ShapeDtypeStruct((ADAPTER_RANK, columns // SHARDS), F32),
            jax.ShapeDtypeStruct((1, 1), F32),
        ),
        in_specs=[SMEM] + [HBM] * 8,
        out_specs=(VMEM, VMEM, VMEM, VMEM),
        scratch_shapes=[
            pltpu.VMEM((rows, model), BF16),
            pltpu.VMEM((rows, 2 * KVH * HD), BF16),
            pltpu.VMEM((2 * KVH, rows, HD), BF16),
            pltpu.VMEM((3 * ADAPTER_RANK, model), BF16),
            pltpu.VMEM((ADAPTER_RANK, columns), BF16),
            pltpu.VMEM(row_table.shape, F32),
            pltpu.VMEM(block_table.shape, F32),
            pltpu.VMEM((KVH, rows, width), BF16),
            pltpu.VMEM((KVH, rows, width), BF16),
            pltpu.VMEM((KVH, GROUP_DEV * rows, 2 * HD), BF16),
            pltpu.VMEM((KVH, GROUP_DEV - 1, rows, 2 * HD), BF16),
            pltpu.VMEM((KVH, GROUP_DEV - 1, rows, 2 * HD), BF16),
            pltpu.VMEM((KVH, rows, 2 * HD), F32),
            pltpu.VMEM((KVH, rows, width), BF16),
            pltpu.VMEM((KVH, rows, 2 * HD), BF16),
            pltpu.VMEM((rows, 2 * KVH * HD), BF16),
            pltpu.VMEM((rows, HD), F32),
            pltpu.VMEM((rows, HD), F32),
            pltpu.VMEM((3 * ADAPTER_RANK, rows), F32),
            pltpu.VMEM((KVH, ADAPTER_RANK, width), F32),
            pltpu.VMEM((ADAPTER_RANK, columns), F32),
            pltpu.VMEM((KVH, ADAPTER_RANK, width), F32),
            pltpu.VMEM((rows, ADAPTER_RANK), F32),
            pltpu.VMEM((2, SHARDS, PIECE, HD), BF16),
            pltpu.VMEM((SHARDS, PIECE, HD), BF16),
            pltpu.VMEM((SHARDS, PIECE, HD), BF16),
            pltpu.VMEM((PLANE, 2, PIECE, HD), BF16),
            pltpu.VMEM((2, PIECE, HD), F32),
            pltpu.VMEM((RING, 2, PIECE, HD), F32),
            pltpu.VMEM((2, PIECE, HD), F32),
            pltpu.VMEM((PLANE, 8, HD), F32),
            pltpu.VMEM((2, 8, HD), F32),
            dma((4,)),
            dma,
            dma,
            dma((2, KVH)),
            dma((KVH, GROUP_DEV - 1)),
            dma((KVH, GROUP_DEV - 1)),
            dma((KVH, GROUP_DEV - 1)),
            dma((KVH, GROUP_DEV - 1)),
            dma,
            dma,
            dma((PLANE,)),
            dma((PLANE,)),
            dma((RING,)),
            dma((RING,)),
            dma,
            dma,
            dma((PLANE,)),
            dma((PLANE,)),
            dma,
            dma,
        ],
        compiler_params=pltpu.CompilerParams(
            collective_id=0, has_side_effects=True, vmem_limit_bytes=48 * 2**20
        ),
        name="attention_and_adapter_gradients",
    )(
        shifted_head_flags,
        *(
            pltpu.with_memory_space_constraint(array, pltpu.HBM)
            for array in (
                normed_layer_input[0],
                query[0],
                saved_key_value[0],
                output_gradient[0],
                adapter_down_weight,
                adapter_up_weight,
                row_table,
                block_table,
            )
        ),
    )
    return (grad_proj[None], grad_down, grad_up, norm[0, 0])


def solution(mesh):
    return jax.shard_map(
        local,
        mesh=mesh,
        in_specs=(
            P("dp", "ctx", None),
            P("dp", "ctx", None),
            P("dp", "ctx", None),
            P("dp", "ctx", None),
            P(),
            P(),
            P(),
        ),
        out_specs=(P("dp", "ctx", None), P(None, "ctx"), P(None, "ctx"), P()),
        check_vma=False,
    )
```

```python
import functools
import math

import jax
import jax.numpy as jnp
import numpy as np
from jax import lax
from jax.experimental import pallas as pl
from jax.experimental.pallas import tpu as pltpu
from jax.sharding import PartitionSpec as P

HQ = 64
KVH = 8
HD = 128
HALF = KVH // 2
GROUP_HEADS = HQ // KVH
ADAPTER_RANK = 8
GROUP_DEV = 4
PACK = 4
SHARDS = 32
PIECE = 48
RING = 4
PLANE = 16

rope_base = 10000.0
adapter_scale = 2.0
SCALE = HD ** (-0.5)
SCALE_LOG2 = SCALE * math.log2(math.e)
MESH = pl.DeviceIdType.MESH
VMEM = pl.BlockSpec(memory_space=pltpu.VMEM)
SMEM = pl.BlockSpec(memory_space=pltpu.SMEM)
HBM = pl.BlockSpec(memory_space=pltpu.HBM)
F32 = jnp.float32
BF16 = jnp.bfloat16


def head_at(flags, position):
    ones = jnp.int32(0)
    head = jnp.int32(0)
    for h in range(KVH):
        flag = jnp.minimum(flags[h], 1)
        here = (1 - flag) * (h - ones) + flag * (HALF + ones)
        head = head + h * (here == position).astype(jnp.int32)
        ones = ones + flag
    return head


def positions_of(flags):
    ones = jnp.int32(0)
    found = []
    for h in range(KVH):
        flag = jnp.minimum(flags[h], 1)
        found.append((1 - flag) * (h - ones) + flag * (HALF + ones))
        ones = ones + flag
    return found


def dot(a, b, ca, cb):
    return lax.dot_general(a, b, (((ca,), (cb,)), ((), ())), preferred_element_type=F32)


def packed_place(shard):
    z, rest = divmod(shard, 8)
    high, x = divmod(rest, 4)
    return (z * 4 + x) * 2 + high


def kernel(
    flags_hbm,
    x_hbm,
    q_hbm,
    kv_hbm,
    g_hbm,
    down_hbm,
    up_hbm,
    row_hbm,
    block_hbm,
    grad_proj,
    down_out,
    up_out,
    norm_out,
    flags,
    xv,
    kv_rows,
    kv,
    down_w,
    up_w,
    row_table,
    block_table,
    qv,
    gv,
    window,
    staged,
    returned,
    own,
    dqs,
    dkv,
    kvn,
    cosines,
    sines,
    low_t,
    up,
    mixed_q,
    packed,
    got1,
    sum1,
    got2,
    sum2,
    got3,
    halves,
    norms,
    quarters,
    flag_sem,
    small_sem,
    x_sem,
    kv_sem,
    in_sem,
    fsend,
    frecv,
    bsend,
    brecv,
    send1,
    recv1,
    send2,
    recv2,
    send3,
    recv3,
    send4,
    recv4,
    send5,
    recv5,
    send6,
    recv6,
):
    rows = q_hbm.shape[0]
    dp = lax.axis_index("dp")
    place = lax.axis_index("ctx")
    count = lax.axis_size("ctx")
    odd = lax.rem(place, 2)
    first_rank = lax.rem(place, GROUP_DEV)
    second_rank = lax.rem(place + 2, GROUP_DEV)
    low_base = jnp.where(first_rank < 2, 0, HALF)
    high_base = HALF - low_base
    core = lax.rem(dp, 2)
    y_low = lax.div(dp, 2)
    y_high = lax.rem(lax.div(place, 4), 2)
    y = y_high * 2 + y_low
    plane = lax.div(place, 8) * 4 + lax.rem(place, 4)
    width = GROUP_HEADS * HD
    width_q = HQ * HD
    width_kv = KVH * HD
    rank_a = ADAPTER_RANK

    flags_in = pltpu.make_async_copy(flags_hbm, flags, flag_sem)
    flags_in.start()
    kv_in = pltpu.make_async_copy(kv_hbm, kv_rows, kv_sem)
    kv_in.start()

    def peer(offset):
        return (dp, lax.rem(place + offset + count, count))

    def device(plane, y, core):
        high, low = lax.div(y, 2), lax.rem(y, 2)
        return (low * 2 + core, lax.div(plane, 4) * 8 + high * 4 + lax.rem(plane, 4))

    def in_plane(step):
        return lax.rem(plane + step, PLANE)

    def in_ring(step):
        return lax.rem(y + step, RING)

    mate = device(plane, y, 1 - core)
    barrier = pltpu.get_barrier_semaphore()

    def greet(target):
        pl.semaphore_signal(barrier, inc=1, device_id=target, device_id_type=MESH)

    for rank in (first_rank, second_rank):
        for step in range(1, GROUP_DEV):
            greet(peer(lax.rem(rank + step, GROUP_DEV) - rank))
    lax.fori_loop(1, PLANE, lambda k, _: (greet(device(in_plane(k), y, core)), 0)[1], 0)
    for step in range(1, RING):
        greet(device(plane, in_ring(step), core))
    greet(mate)

    copies_in = []
    for h in range(KVH):
        part = slice(h * width, (h + 1) * width)
        copies_in.append(pltpu.make_async_copy(q_hbm.at[:, part], qv.at[h], in_sem.at[0, h]))
        copies_in.append(pltpu.make_async_copy(g_hbm.at[:, part], gv.at[h], in_sem.at[1, h]))
    small_in = [
        pltpu.make_async_copy(source, target, small_sem.at[i])
        for i, (source, target) in enumerate(
            [(row_hbm, row_table), (block_hbm, block_table), (up_hbm, up_w), (down_hbm, down_w)]
        )
    ]
    x_in = pltpu.make_async_copy(x_hbm, xv, x_sem)
    flags_in.wait()
    kv_in.wait()
    for copy in copies_in + small_in + [x_in]:
        copy.start()
    for h in range(2 * KVH):
        kv[h] = kv_rows[:, h * HD : (h + 1) * HD]
    for c in range(KVH):
        rank = first_rank if c < HALF else second_rank
        head = head_at(flags, c)
        slot = pl.ds(pl.multiple_of(rank * rows, rows), rows)
        window[c, slot, 0:HD] = kv[head]
        window[c, slot, HD : 2 * HD] = kv[head + KVH]

    pl.semaphore_wait(barrier, 2 * (GROUP_DEV - 1) + PLANE - 1 + RING - 1 + 1)

    def forward(c, rank, distance):
        part = window.at[c, rank * rows : (rank + 1) * rows]
        return pltpu.make_async_remote_copy(
            src_ref=part,
            dst_ref=part,
            send_sem=fsend.at[c, distance - 1],
            recv_sem=frecv.at[c, rank],
            device_id=peer(distance),
            device_id_type=MESH,
        )

    def back(c, rank, target):
        return pltpu.make_async_remote_copy(
            src_ref=staged.at[c, target],
            dst_ref=returned.at[c, rank - 1],
            send_sem=bsend.at[c, target],
            recv_sem=brecv.at[c, rank - 1],
            device_id=peer(target - rank),
            device_id_type=MESH,
        )

    def each_head(step, start=0, stop=HALF):
        lax.fori_loop(start, stop, lambda i, _: (step(i), 0)[1], 0)

    def sends(low, high):
        if low == 0:
            each_head(lambda i: forward(low_base + i, 0, 1).start(), 0, 2)

        def send_all(i):
            for base, rank in ((low_base, low), (high_base, high)):
                for distance in range(2 if rank == 0 else 1, GROUP_DEV - rank):
                    forward(base + i, rank, distance).start()

        each_head(send_all)
        if low == 0:
            each_head(lambda i: forward(low_base + i, 0, 1).start(), 2, HALF)

    pl.when(odd == 0)(lambda: sends(0, 2))
    pl.when(odd == 1)(lambda: sends(1, 3))

    for copy in small_in:
        copy.wait()
    block_cos, block_sin = block_table[0, pl.ds(place, 1)], block_table[1, pl.ds(place, 1)]
    row_cos, row_sin = row_table[0], row_table[1]
    cosines[...] = block_cos * row_cos - block_sin * row_sin
    sines[...] = block_sin * row_cos + block_cos * row_sin
    for copy in copies_in:
        copy.wait()
    x_in.wait()
    low_t[...] = jnp.transpose(dot(xv[...], down_w[...], 1, 1))

    def low_of(segment):
        return low_t[segment * rank_a : (segment + 1) * rank_a].astype(BF16)

    def work(c, rank):
        blocks = rank + 1
        span = blocks * rows
        for source in range(rank):
            forward(c, source, rank - source).wait_recv()
        head = head_at(flags, c)
        keys = window[c, 0:span, 0:HD]
        values = window[c, 0:span, HD : 2 * HD]
        packed_rows = PACK * rows
        row = lax.broadcasted_iota(jnp.int32, (rows, packed_rows), 0)
        column = lax.rem(lax.broadcasted_iota(jnp.int32, (rows, packed_rows), 1), rows)
        allowed = row <= column
        key_sum, value_sum = None, None
        for j in range(GROUP_HEADS // PACK):

            def stacked(ref):
                return jnp.concatenate(
                    [ref[head, :, (j * PACK + t) * HD : (j * PACK + t + 1) * HD] for t in range(PACK)],
                    axis=0,
                )

            queries = stacked(qv)
            grads = stacked(gv)
            scores = dot(keys, queries, 1, 1)
            grad_probs = dot(values, grads, 1, 1)
            last = jnp.where(allowed, scores[span - rows :], -1e30)
            scores = jnp.concatenate([scores[: span - rows], last], axis=0) if rank else last
            peak = jnp.max(scores, axis=0, keepdims=True)
            weights = jnp.exp2((scores - peak) * SCALE_LOG2)
            probs = weights * (1.0 / jnp.sum(weights, axis=0, keepdims=True))
            inner = jnp.sum(probs * grad_probs, axis=0, keepdims=True)
            probs_low = probs.astype(BF16)
            grad_scores = (probs * (grad_probs - inner)).astype(BF16)
            value_term = dot(probs_low, grads, 1, 0)
            key_term = dot(grad_scores, queries, 1, 0)
            value_sum = value_term if value_sum is None else value_sum + value_term
            key_sum = key_term if key_sum is None else key_sum + key_term
            grad_query = dot(grad_scores, keys, 0, 0)
            for t in range(PACK):
                piece = grad_query[t * rows : (t + 1) * rows]
                piece = piece * cosines[...] + pltpu.roll(piece, HD // 2, 1) * sines[...]
                lanes = (j * PACK + t) * HD
                dqs[c, :, lanes : lanes + HD] = piece.astype(BF16)
        for target in range(rank):
            part = slice(target * rows, (target + 1) * rows)
            staged[c, target, :, 0:HD] = key_sum[part].astype(BF16)
            staged[c, target, :, HD : 2 * HD] = value_sum[part].astype(BF16)
            back(c, rank, target).start()
        own[c, :, 0:HD] = key_sum[span - rows :]
        own[c, :, HD : 2 * HD] = value_sum[span - rows :]

    def finish(c, rank):
        total = own[c]
        for sender in range(rank + 1, GROUP_DEV):
            back(c, sender, rank).wait_recv()
            total = total + returned[c, sender - 1].astype(F32)
        keys = total[:, 0:HD]
        keys = keys * cosines[...] + pltpu.roll(keys, HD // 2, 1) * sines[...]
        dkv[c, :, 0:HD] = keys.astype(BF16)
        dkv[c, :, HD : 2 * HD] = total[:, HD : 2 * HD].astype(BF16)

    def phase(low, high):
        early = HALF if low == 0 else 2

        def step(t):
            is_high = jnp.logical_and(t >= early, t < early + HALF)
            pl.when(is_high)(lambda: work(high_base + t - early, high))
            pl.when(jnp.logical_not(is_high))(
                lambda: work(low_base + jnp.where(t < early, t, t - HALF), low)
            )

        each_head(step, 0, KVH)

    pl.when(odd == 0)(lambda: phase(0, 2))
    pl.when(odd == 1)(lambda: phase(1, 3))

    position = positions_of(flags)
    mixed_sum = None
    for h in range(KVH):
        part = slice(h * width, (h + 1) * width)
        block = dqs[position[h]]
        grad_proj[:, part] = block
        up[:, part] = adapter_scale * dot(low_of(0), block, 1, 0)
        term = dot(block, up_w[:, part], 1, 1)
        mixed_sum = term if mixed_sum is None else mixed_sum + term
    mixed_q[...] = mixed_sum

    def collect(low, high):
        def last(i):
            finish(high_base + i, high)
            finish(low_base + i, low)

        each_head(last)

    pl.when(odd == 0)(lambda: collect(0, 2))
    pl.when(odd == 1)(lambda: collect(1, 3))

    for h in range(KVH):
        kvn[:, h * HD : (h + 1) * HD] = dkv[position[h], :, 0:HD]
        kvn[:, width_kv + h * HD : width_kv + (h + 1) * HD] = dkv[position[h], :, HD : 2 * HD]
    grad_proj[:, width_q : width_q + 2 * width_kv] = kvn[...]
    up[:, width_q : width_q + width_kv] = adapter_scale * dot(low_of(1), kvn[:, 0:width_kv], 1, 0)
    up[:, width_q + width_kv :] = adapter_scale * dot(low_of(2), kvn[:, width_kv:], 1, 0)
    mixed_k = dot(kvn[:, 0:width_kv], up_w[:, width_q : width_q + width_kv], 1, 1)
    mixed_v = dot(kvn[:, width_kv:], up_w[:, width_q + width_kv :], 1, 1)
    mixed = jnp.transpose(jnp.concatenate([mixed_q[...], mixed_k, mixed_v], axis=1)).astype(BF16)
    down_width = xv.shape[1] // SHARDS
    up_width = up.shape[1] // SHARDS
    zeros = jnp.zeros((8, HD), F32)
    for shard in range(SHARDS):
        down = adapter_scale * dot(mixed, xv[:, shard * down_width : (shard + 1) * down_width], 1, 0)
        mine = up[:, shard * up_width : (shard + 1) * up_width]
        rest = jnp.concatenate(
            [mine[:, 2 * HD :], jnp.zeros((8, 3 * HD - up_width), F32)], axis=1
        )
        at = packed_place(shard)
        packed[0, at] = jnp.concatenate([down[:, 0:HD], mine[:, 0:HD], rest, zeros], 0).astype(BF16)
        packed[1, at] = jnp.concatenate(
            [down[:, HD:], mine[:, HD : 2 * HD], zeros, zeros], 0
        ).astype(BF16)

    def remote(src, dst, send, recv, target):
        return pltpu.make_async_remote_copy(
            src_ref=src,
            dst_ref=dst,
            send_sem=send,
            recv_sem=recv,
            device_id=target,
            device_id_type=MESH,
        )

    first = remote(packed.at[1 - core], got1, send1, recv1, mate)
    first.start()
    first.wait_recv()

    def both(t):
        part = pl.ds(2 * t, 2)
        return packed[core, part].astype(F32) + got1[part].astype(F32)

    def second(k):
        t = in_plane(k)
        part = pl.ds(2 * t, 2)
        return remote(
            sum1.at[part], got2.at[plane], send2.at[k], recv2.at[plane], device(t, y, core)
        )

    def send_second(k, _):
        t = in_plane(k)
        sum1[pl.ds(2 * t, 2)] = both(t).astype(BF16)
        second(k).start()
        return 0

    lax.fori_loop(1, PLANE, send_second, 0)
    total = both(plane)

    def add_second(k, total):
        source = in_plane(PLANE - k)
        remote(
            sum1.at[pl.ds(0, 2)], got2.at[source], send2.at[k], recv2.at[source], mate
        ).wait_recv()
        return total + got2[source].astype(F32)

    sum2[...] = lax.fori_loop(1, PLANE, add_second, total)

    got3[y] = sum2[...]

    def third(step):
        return remote(
            got3.at[y],
            got3.at[y],
            send3.at[step],
            recv3.at[y],
            device(plane, in_ring(step), core),
        )

    for step in range(1, RING):
        third(step).start()
    for step in range(1, RING):
        source = in_ring(step)
        remote(got3.at[source], got3.at[source], send3.at[step], recv3.at[source], mate).wait_recv()
    whole = got3[0] + got3[1] + got3[2] + got3[3]
    sum2[...] = whole
    halves[core] = sum2[y_high]
    fourth = remote(halves.at[core], halves.at[core], send4, recv4, mate)
    squares = whole * whole
    norms[plane] = functools.reduce(
        lambda a, b: a + b,
        [squares[h, 8 * r : 8 * (r + 1)] for h in range(2) for r in range(PIECE // 8)],
    )

    def fifth(k):
        return remote(
            norms.at[plane], norms.at[plane], send5.at[k], recv5.at[plane], device(in_plane(k), y, core)
        )

    def fifth_arrival(k):
        source = in_plane(k)
        return remote(norms.at[source], norms.at[source], send5.at[k], recv5.at[source], mate)

    lax.fori_loop(1, PLANE, lambda k, _: (fifth(k).start(), 0)[1], 0)
    fourth.start()
    remote(halves.at[core], halves.at[1 - core], send4, recv4, mate).wait_recv()
    down_out[:, 0:HD] = halves[0, 0:24]
    down_out[:, HD : 2 * HD] = halves[1, 0:24]
    up_out[:, 0:HD] = halves[0, 24:32]
    up_out[:, HD : 2 * HD] = halves[1, 24:32]
    up_out[:, 2 * HD :] = halves[0, 32:40, 0 : up_out.shape[1] - 2 * HD]
    lax.fori_loop(1, PLANE, lambda k, _: (fifth_arrival(k).wait_recv(), 0)[1], 0)
    quarters[core] = jnp.sum(norms[...], axis=0)
    sixth = remote(quarters.at[core], quarters.at[core], send6, recv6, mate)
    sixth.start()
    remote(quarters.at[1 - core], quarters.at[1 - core], send6, recv6, mate).wait_recv()
    everything = jnp.sum(quarters[0] + quarters[1], keepdims=True)
    norm_out[...] = jnp.broadcast_to(jnp.sqrt(everything), norm_out.shape)

    first.wait_send()
    fourth.wait_send()
    lax.fori_loop(1, PLANE, lambda k, _: (second(k).wait_send(), 0)[1], 0)
    lax.fori_loop(1, PLANE, lambda k, _: (fifth(k).wait_send(), 0)[1], 0)
    for step in range(1, 4):
        third(step).wait_send()
    sixth.wait_send()

    def drain(low, high):
        def wait(i):
            for base, rank in ((low_base, low), (high_base, high)):
                for distance in range(1, GROUP_DEV - rank):
                    forward(base + i, rank, distance).wait_send()
                for target in range(rank):
                    back(base + i, rank, target).wait_send()

        each_head(wait)

    pl.when(odd == 0)(lambda: drain(0, 2))
    pl.when(odd == 1)(lambda: drain(1, 3))


def rotary_constants(rows, blocks):
    freqs = rope_base ** (-2.0 * np.arange(HD // 2) / HD)

    def table(positions, scale):
        angles = positions[:, None] * freqs[None, :]
        cosines, sines = np.cos(angles), np.sin(angles)
        both = np.stack(
            [np.concatenate([cosines, cosines], 1), np.concatenate([sines, -sines], 1)]
        )
        return jnp.asarray((both * scale).astype(np.float32))

    return table(np.arange(rows), 1.0), table(np.arange(blocks) * rows, SCALE)


def local(
    normed_layer_input,
    query,
    saved_key_value,
    output_gradient,
    adapter_down_weight,
    adapter_up_weight,
    shifted_head_flags,
):
    rows, model = normed_layer_input.shape[1:]
    columns = adapter_up_weight.shape[1]
    width = GROUP_HEADS * HD
    row_table, block_table = rotary_constants(rows, lax.axis_size("ctx"))
    dma = pltpu.SemaphoreType.DMA
    grad_proj, grad_down, grad_up, norm = pl.pallas_call(
        kernel,
        out_shape=(
            pltpu.VMEM((rows, columns), BF16),
            jax.ShapeDtypeStruct((3 * ADAPTER_RANK, model // SHARDS), F32),
            jax.ShapeDtypeStruct((ADAPTER_RANK, columns // SHARDS), F32),
            jax.ShapeDtypeStruct((8, HD), F32),
        ),
        in_specs=[HBM] * 9,
        out_specs=(VMEM, VMEM, VMEM, VMEM),
        scratch_shapes=[
            pltpu.SMEM((KVH,), jnp.int32),
            pltpu.VMEM((rows, model), BF16),
            pltpu.VMEM((rows, 2 * KVH * HD), BF16),
            pltpu.VMEM((2 * KVH, rows, HD), BF16),
            pltpu.VMEM((3 * ADAPTER_RANK, model), BF16),
            pltpu.VMEM((ADAPTER_RANK, columns), BF16),
            pltpu.VMEM(row_table.shape, F32),
            pltpu.VMEM(block_table.shape, F32),
            pltpu.VMEM((KVH, rows, width), BF16),
            pltpu.VMEM((KVH, rows, width), BF16),
            pltpu.VMEM((KVH, GROUP_DEV * rows, 2 * HD), BF16),
            pltpu.VMEM((KVH, GROUP_DEV - 1, rows, 2 * HD), BF16),
            pltpu.VMEM((KVH, GROUP_DEV - 1, rows, 2 * HD), BF16),
            pltpu.VMEM((KVH, rows, 2 * HD), F32),
            pltpu.VMEM((KVH, rows, width), BF16),
            pltpu.VMEM((KVH, rows, 2 * HD), BF16),
            pltpu.VMEM((rows, 2 * KVH * HD), BF16),
            pltpu.VMEM((rows, HD), F32),
            pltpu.VMEM((rows, HD), F32),
            pltpu.VMEM((3 * ADAPTER_RANK, rows), F32),
            pltpu.VMEM((ADAPTER_RANK, columns), F32),
            pltpu.VMEM((rows, ADAPTER_RANK), F32),
            pltpu.VMEM((2, SHARDS, PIECE, HD), BF16),
            pltpu.VMEM((SHARDS, PIECE, HD), BF16),
            pltpu.VMEM((SHARDS, PIECE, HD), BF16),
            pltpu.VMEM((PLANE, 2, PIECE, HD), BF16),
            pltpu.VMEM((2, PIECE, HD), F32),
            pltpu.VMEM((RING, 2, PIECE, HD), F32),
            pltpu.VMEM((2, PIECE, HD), F32),
            pltpu.VMEM((PLANE, 8, HD), F32),
            pltpu.VMEM((2, 8, HD), F32),
            dma,
            dma((4,)),
            dma,
            dma,
            dma((2, KVH)),
            dma((KVH, GROUP_DEV - 1)),
            dma((KVH, GROUP_DEV - 1)),
            dma((KVH, GROUP_DEV - 1)),
            dma((KVH, GROUP_DEV - 1)),
            dma,
            dma,
            dma((PLANE,)),
            dma((PLANE,)),
            dma((RING,)),
            dma((RING,)),
            dma,
            dma,
            dma((PLANE,)),
            dma((PLANE,)),
            dma,
            dma,
        ],
        compiler_params=pltpu.CompilerParams(
            collective_id=0, has_side_effects=True, vmem_limit_bytes=48 * 2**20
        ),
        name="attention_and_adapter_gradients",
    )(
        *(
            pltpu.with_memory_space_constraint(array, pltpu.HBM)
            for array in (
                shifted_head_flags,
                normed_layer_input[0],
                query[0],
                saved_key_value[0],
                output_gradient[0],
                adapter_down_weight,
                adapter_up_weight,
                row_table,
                block_table,
            )
        ),
    )
    return (grad_proj[None], grad_down, grad_up, norm[0, 0])


def solution(mesh):
    return jax.shard_map(
        local,
        mesh=mesh,
        in_specs=(
            P("dp", "ctx", None),
            P("dp", "ctx", None),
            P("dp", "ctx", None),
            P("dp", "ctx", None),
            P(),
            P(),
            P(),
        ),
        out_specs=(P("dp", "ctx", None), P(None, "ctx"), P(None, "ctx"), P()),
        check_vma=False,
    )
```

```python
import functools
import math

import jax
import jax.numpy as jnp
import numpy as np
from jax import lax
from jax.experimental import pallas as pl
from jax.experimental.pallas import tpu as pltpu
from jax.sharding import PartitionSpec as P

HQ = 64
KVH = 8
HD = 128
HALF = KVH // 2
GROUP_HEADS = HQ // KVH
ADAPTER_RANK = 8
GROUP_DEV = 4
PACK = 4
SHARDS = 32
PIECE = 48
RING = 4
PLANE = 16

rope_base = 10000.0
adapter_scale = 2.0
SCALE = HD ** (-0.5)
SCALE_LOG2 = SCALE * math.log2(math.e)
MESH = pl.DeviceIdType.MESH
VMEM = pl.BlockSpec(memory_space=pltpu.VMEM)
SMEM = pl.BlockSpec(memory_space=pltpu.SMEM)
HBM = pl.BlockSpec(memory_space=pltpu.HBM)
F32 = jnp.float32
BF16 = jnp.bfloat16


def head_at(flags, position):
    ones = jnp.int32(0)
    head = jnp.int32(0)
    for h in range(KVH):
        flag = jnp.minimum(flags[h], 1)
        here = (1 - flag) * (h - ones) + flag * (HALF + ones)
        head = head + h * (here == position).astype(jnp.int32)
        ones = ones + flag
    return head


def positions_of(flags):
    ones = jnp.int32(0)
    found = []
    for h in range(KVH):
        flag = jnp.minimum(flags[h], 1)
        found.append((1 - flag) * (h - ones) + flag * (HALF + ones))
        ones = ones + flag
    return found


def dot(a, b, ca, cb):
    return lax.dot_general(a, b, (((ca,), (cb,)), ((), ())), preferred_element_type=F32)


def packed_place(shard):
    z, rest = divmod(shard, 8)
    high, x = divmod(rest, 4)
    return (z * 4 + x) * 2 + high


def kernel(
    flags_hbm,
    x_hbm,
    q_hbm,
    kv_hbm,
    g_hbm,
    down_hbm,
    up_hbm,
    row_hbm,
    block_hbm,
    grad_proj,
    down_out,
    up_out,
    norm_out,
    flags,
    xv,
    kv_rows,
    kv,
    down_w,
    up_w,
    row_table,
    block_table,
    qv,
    gv,
    window,
    staged,
    returned,
    own,
    dqs,
    dkv,
    kvn,
    cosines,
    sines,
    low_t,
    up,
    mixed_q,
    packed,
    got1,
    sum1,
    got2,
    sum2,
    got3,
    halves,
    norms,
    quarters,
    flag_sem,
    small_sem,
    x_sem,
    kv_sem,
    in_sem,
    fsend,
    frecv,
    bsend,
    brecv,
    send1,
    recv1,
    send2,
    recv2,
    send3,
    recv3,
    send4,
    recv4,
    send5,
    recv5,
    send6,
    recv6,
):
    rows = q_hbm.shape[0]
    dp = lax.axis_index("dp")
    place = lax.axis_index("ctx")
    count = lax.axis_size("ctx")
    odd = lax.rem(place, 2)
    first_rank = lax.rem(place, GROUP_DEV)
    second_rank = lax.rem(place + 2, GROUP_DEV)
    low_base = jnp.where(first_rank < 2, 0, HALF)
    high_base = HALF - low_base
    core = lax.rem(dp, 2)
    y_low = lax.div(dp, 2)
    y_high = lax.rem(lax.div(place, 4), 2)
    y = y_high * 2 + y_low
    plane = lax.div(place, 8) * 4 + lax.rem(place, 4)
    width = GROUP_HEADS * HD
    width_q = HQ * HD
    width_kv = KVH * HD
    rank_a = ADAPTER_RANK

    flags_in = pltpu.make_async_copy(flags_hbm, flags, flag_sem)
    flags_in.start()
    kv_in = pltpu.make_async_copy(kv_hbm, kv_rows, kv_sem)
    kv_in.start()

    def peer(offset):
        return (dp, lax.rem(place + offset + count, count))

    def device(plane, y, core):
        high, low = lax.div(y, 2), lax.rem(y, 2)
        return (low * 2 + core, lax.div(plane, 4) * 8 + high * 4 + lax.rem(plane, 4))

    def in_plane(step):
        return lax.rem(plane + step, PLANE)

    def in_ring(step):
        return lax.rem(y + step, RING)

    mate = device(plane, y, 1 - core)
    barrier = pltpu.get_barrier_semaphore()

    def greet(target):
        pl.semaphore_signal(barrier, inc=1, device_id=target, device_id_type=MESH)

    for rank in (first_rank, second_rank):
        for step in range(1, GROUP_DEV):
            greet(peer(lax.rem(rank + step, GROUP_DEV) - rank))
    lax.fori_loop(1, PLANE, lambda k, _: (greet(device(in_plane(k), y, core)), 0)[1], 0)
    for step in range(1, RING):
        greet(device(plane, in_ring(step), core))
    greet(mate)

    copies_in = []
    for h in range(KVH):
        part = slice(h * width, (h + 1) * width)
        copies_in.append(pltpu.make_async_copy(q_hbm.at[:, part], qv.at[h], in_sem.at[0, h]))
        copies_in.append(pltpu.make_async_copy(g_hbm.at[:, part], gv.at[h], in_sem.at[1, h]))
    small_in = [
        pltpu.make_async_copy(source, target, small_sem.at[i])
        for i, (source, target) in enumerate(
            [(row_hbm, row_table), (block_hbm, block_table), (up_hbm, up_w), (down_hbm, down_w)]
        )
    ]
    x_in = pltpu.make_async_copy(x_hbm, xv, x_sem)
    flags_in.wait()
    kv_in.wait()
    for copy in copies_in + small_in + [x_in]:
        copy.start()
    for h in range(2 * KVH):
        kv[h] = kv_rows[:, h * HD : (h + 1) * HD]
    for c in range(KVH):
        rank = first_rank if c < HALF else second_rank
        head = head_at(flags, c)
        slot = pl.ds(pl.multiple_of(rank * rows, rows), rows)
        window[c, slot, 0:HD] = kv[head]
        window[c, slot, HD : 2 * HD] = kv[head + KVH]

    pl.semaphore_wait(barrier, 2 * (GROUP_DEV - 1) + PLANE - 1 + RING - 1 + 1)

    def forward(c, rank, distance):
        part = window.at[c, rank * rows : (rank + 1) * rows]
        return pltpu.make_async_remote_copy(
            src_ref=part,
            dst_ref=part,
            send_sem=fsend.at[c, distance - 1],
            recv_sem=frecv.at[c, rank],
            device_id=peer(distance),
            device_id_type=MESH,
        )

    def back(c, rank, target):
        return pltpu.make_async_remote_copy(
            src_ref=staged.at[c, target],
            dst_ref=returned.at[c, rank - 1],
            send_sem=bsend.at[c, target],
            recv_sem=brecv.at[c, rank - 1],
            device_id=peer(target - rank),
            device_id_type=MESH,
        )

    def each_head(step, start=0, stop=HALF):
        lax.fori_loop(start, stop, lambda i, _: (step(i), 0)[1], 0)

    def sends(low, high):
        if low == 0:
            each_head(lambda i: forward(low_base + i, 0, 1).start(), 0, 2)

        def send_all(i):
            for base, rank in ((low_base, low), (high_base, high)):
                for distance in range(2 if rank == 0 else 1, GROUP_DEV - rank):
                    forward(base + i, rank, distance).start()

        each_head(send_all)
        if low == 0:
            each_head(lambda i: forward(low_base + i, 0, 1).start(), 2, HALF)

    pl.when(odd == 0)(lambda: sends(0, 2))
    pl.when(odd == 1)(lambda: sends(1, 3))

    for copy in small_in:
        copy.wait()
    block_cos, block_sin = block_table[0, pl.ds(place, 1)], block_table[1, pl.ds(place, 1)]
    row_cos, row_sin = row_table[0], row_table[1]
    cosines[...] = block_cos * row_cos - block_sin * row_sin
    sines[...] = block_sin * row_cos + block_cos * row_sin
    for copy in copies_in:
        copy.wait()

    def low_of(segment):
        return low_t[segment * rank_a : (segment + 1) * rank_a].astype(BF16)

    def work(c, rank):
        blocks = rank + 1
        span = blocks * rows
        for source in range(rank):
            forward(c, source, rank - source).wait_recv()
        head = head_at(flags, c)
        keys = window[c, 0:span, 0:HD]
        values = window[c, 0:span, HD : 2 * HD]
        packed_rows = PACK * rows
        row = lax.broadcasted_iota(jnp.int32, (rows, packed_rows), 0)
        column = lax.rem(lax.broadcasted_iota(jnp.int32, (rows, packed_rows), 1), rows)
        allowed = row <= column
        key_sum, value_sum = None, None
        for j in range(GROUP_HEADS // PACK):

            def stacked(ref):
                return jnp.concatenate(
                    [ref[head, :, (j * PACK + t) * HD : (j * PACK + t + 1) * HD] for t in range(PACK)],
                    axis=0,
                )

            queries = stacked(qv)
            grads = stacked(gv)
            scores = dot(keys, queries, 1, 1)
            grad_probs = dot(values, grads, 1, 1)
            last = jnp.where(allowed, scores[span - rows :], -1e30)
            scores = jnp.concatenate([scores[: span - rows], last], axis=0) if rank else last
            peak = jnp.max(scores, axis=0, keepdims=True)
            weights = jnp.exp2((scores - peak) * SCALE_LOG2)
            probs = weights * (1.0 / jnp.sum(weights, axis=0, keepdims=True))
            inner = jnp.sum(probs * grad_probs, axis=0, keepdims=True)
            probs_low = probs.astype(BF16)
            grad_scores = (probs * (grad_probs - inner)).astype(BF16)
            value_term = dot(probs_low, grads, 1, 0)
            key_term = dot(grad_scores, queries, 1, 0)
            value_sum = value_term if value_sum is None else value_sum + value_term
            key_sum = key_term if key_sum is None else key_sum + key_term
            grad_query = dot(grad_scores, keys, 0, 0)
            for t in range(PACK):
                piece = grad_query[t * rows : (t + 1) * rows]
                piece = piece * cosines[...] + pltpu.roll(piece, HD // 2, 1) * sines[...]
                lanes = (j * PACK + t) * HD
                dqs[c, :, lanes : lanes + HD] = piece.astype(BF16)
        for target in range(rank):
            part = slice(target * rows, (target + 1) * rows)
            staged[c, target, :, 0:HD] = key_sum[part].astype(BF16)
            staged[c, target, :, HD : 2 * HD] = value_sum[part].astype(BF16)
            back(c, rank, target).start()
        own[c, :, 0:HD] = key_sum[span - rows :]
        own[c, :, HD : 2 * HD] = value_sum[span - rows :]

    def finish(c, rank):
        total = own[c]
        for sender in range(rank + 1, GROUP_DEV):
            back(c, sender, rank).wait_recv()
            total = total + returned[c, sender - 1].astype(F32)
        keys = total[:, 0:HD]
        keys = keys * cosines[...] + pltpu.roll(keys, HD // 2, 1) * sines[...]
        dkv[c, :, 0:HD] = keys.astype(BF16)
        dkv[c, :, HD : 2 * HD] = total[:, HD : 2 * HD].astype(BF16)

    def phase(low, high):
        early = HALF if low == 0 else 2

        def step(t):
            is_high = jnp.logical_and(t >= early, t < early + HALF)
            pl.when(is_high)(lambda: work(high_base + t - early, high))
            pl.when(jnp.logical_not(is_high))(
                lambda: work(low_base + jnp.where(t < early, t, t - HALF), low)
            )

        each_head(step, 0, KVH)

    pl.when(odd == 0)(lambda: phase(0, 2))
    pl.when(odd == 1)(lambda: phase(1, 3))

    position = positions_of(flags)
    x_in.wait()
    low_t[...] = jnp.transpose(dot(xv[...], down_w[...], 1, 1))
    mixed_sum = None
    for h in range(KVH):
        part = slice(h * width, (h + 1) * width)
        block = dqs[position[h]]
        grad_proj[:, part] = block
        up[:, part] = adapter_scale * dot(low_of(0), block, 1, 0)
        term = dot(block, up_w[:, part], 1, 1)
        mixed_sum = term if mixed_sum is None else mixed_sum + term
    mixed_q[...] = mixed_sum

    def collect(low, high):
        def last(i):
            finish(high_base + i, high)
            finish(low_base + i, low)

        each_head(last)

    pl.when(odd == 0)(lambda: collect(0, 2))
    pl.when(odd == 1)(lambda: collect(1, 3))

    for h in range(KVH):
        kvn[:, h * HD : (h + 1) * HD] = dkv[position[h], :, 0:HD]
        kvn[:, width_kv + h * HD : width_kv + (h + 1) * HD] = dkv[position[h], :, HD : 2 * HD]
    grad_proj[:, width_q : width_q + 2 * width_kv] = kvn[...]
    up[:, width_q : width_q + width_kv] = adapter_scale * dot(low_of(1), kvn[:, 0:width_kv], 1, 0)
    up[:, width_q + width_kv :] = adapter_scale * dot(low_of(2), kvn[:, width_kv:], 1, 0)
    mixed_k = dot(kvn[:, 0:width_kv], up_w[:, width_q : width_q + width_kv], 1, 1)
    mixed_v = dot(kvn[:, width_kv:], up_w[:, width_q + width_kv :], 1, 1)
    mixed = jnp.transpose(jnp.concatenate([mixed_q[...], mixed_k, mixed_v], axis=1)).astype(BF16)
    down_width = xv.shape[1] // SHARDS
    up_width = up.shape[1] // SHARDS
    zeros = jnp.zeros((8, HD), F32)
    def remote(src, dst, send, recv, target):
        return pltpu.make_async_remote_copy(
            src_ref=src,
            dst_ref=dst,
            send_sem=send,
            recv_sem=recv,
            device_id=target,
            device_id_type=MESH,
        )

    def first(chunk):
        part = slice(chunk * PLANE, (chunk + 1) * PLANE)
        return remote(
            packed.at[1 - core, part], got1.at[part], send1.at[chunk], recv1.at[chunk], mate
        )

    for shard in range(SHARDS):
        down = adapter_scale * dot(mixed, xv[:, shard * down_width : (shard + 1) * down_width], 1, 0)
        mine = up[:, shard * up_width : (shard + 1) * up_width]
        rest = jnp.concatenate(
            [mine[:, 2 * HD :], jnp.zeros((8, 3 * HD - up_width), F32)], axis=1
        )
        at = packed_place(shard)
        packed[0, at] = jnp.concatenate([down[:, 0:HD], mine[:, 0:HD], rest, zeros], 0).astype(BF16)
        packed[1, at] = jnp.concatenate(
            [down[:, HD:], mine[:, HD : 2 * HD], zeros, zeros], 0
        ).astype(BF16)
        if shard % PLANE == PLANE - 1:
            first(shard // PLANE).start()

    for chunk in range(2):
        first(chunk).wait_recv()

    def both(t):
        part = pl.ds(2 * t, 2)
        return packed[core, part].astype(F32) + got1[part].astype(F32)

    def second(k):
        t = in_plane(k)
        part = pl.ds(2 * t, 2)
        return remote(
            sum1.at[part], got2.at[plane], send2.at[k], recv2.at[plane], device(t, y, core)
        )

    def send_second(k, _):
        t = in_plane(k)
        sum1[pl.ds(2 * t, 2)] = both(t).astype(BF16)
        second(k).start()
        return 0

    lax.fori_loop(1, PLANE, send_second, 0)
    total = both(plane)

    def add_second(k, total):
        source = in_plane(PLANE - k)
        remote(
            sum1.at[pl.ds(0, 2)], got2.at[source], send2.at[k], recv2.at[source], mate
        ).wait_recv()
        return total + got2[source].astype(F32)

    sum2[...] = lax.fori_loop(1, PLANE, add_second, total)

    got3[y] = sum2[...]

    def third(step):
        return remote(
            got3.at[y],
            got3.at[y],
            send3.at[step],
            recv3.at[y],
            device(plane, in_ring(step), core),
        )

    for step in range(1, RING):
        third(step).start()
    for step in range(1, RING):
        source = in_ring(step)
        remote(got3.at[source], got3.at[source], send3.at[step], recv3.at[source], mate).wait_recv()
    whole = got3[0] + got3[1] + got3[2] + got3[3]
    sum2[...] = whole
    halves[core] = sum2[y_high]
    fourth = remote(halves.at[core], halves.at[core], send4, recv4, mate)
    squares = whole * whole
    norms[plane] = functools.reduce(
        lambda a, b: a + b,
        [squares[h, 8 * r : 8 * (r + 1)] for h in range(2) for r in range(PIECE // 8)],
    )

    def fifth(k):
        return remote(
            norms.at[plane], norms.at[plane], send5.at[k], recv5.at[plane], device(in_plane(k), y, core)
        )

    def fifth_arrival(k):
        source = in_plane(k)
        return remote(norms.at[source], norms.at[source], send5.at[k], recv5.at[source], mate)

    lax.fori_loop(1, PLANE, lambda k, _: (fifth(k).start(), 0)[1], 0)
    fourth.start()
    remote(halves.at[core], halves.at[1 - core], send4, recv4, mate).wait_recv()
    down_out[:, 0:HD] = halves[0, 0:24]
    down_out[:, HD : 2 * HD] = halves[1, 0:24]
    up_out[:, 0:HD] = halves[0, 24:32]
    up_out[:, HD : 2 * HD] = halves[1, 24:32]
    up_out[:, 2 * HD :] = halves[0, 32:40, 0 : up_out.shape[1] - 2 * HD]
    lax.fori_loop(1, PLANE, lambda k, _: (fifth_arrival(k).wait_recv(), 0)[1], 0)
    quarters[core] = jnp.sum(norms[...], axis=0)
    sixth = remote(quarters.at[core], quarters.at[core], send6, recv6, mate)
    sixth.start()
    remote(quarters.at[1 - core], quarters.at[1 - core], send6, recv6, mate).wait_recv()
    everything = jnp.sum(quarters[0] + quarters[1], keepdims=True)
    norm_out[...] = jnp.broadcast_to(jnp.sqrt(everything), norm_out.shape)

    for chunk in range(2):
        first(chunk).wait_send()
    fourth.wait_send()
    lax.fori_loop(1, PLANE, lambda k, _: (second(k).wait_send(), 0)[1], 0)
    lax.fori_loop(1, PLANE, lambda k, _: (fifth(k).wait_send(), 0)[1], 0)
    for step in range(1, 4):
        third(step).wait_send()
    sixth.wait_send()

    def drain(low, high):
        def wait(i):
            for base, rank in ((low_base, low), (high_base, high)):
                for distance in range(1, GROUP_DEV - rank):
                    forward(base + i, rank, distance).wait_send()
                for target in range(rank):
                    back(base + i, rank, target).wait_send()

        each_head(wait)

    pl.when(odd == 0)(lambda: drain(0, 2))
    pl.when(odd == 1)(lambda: drain(1, 3))


def rotary_constants(rows, blocks):
    freqs = rope_base ** (-2.0 * np.arange(HD // 2) / HD)

    def table(positions, scale):
        angles = positions[:, None] * freqs[None, :]
        cosines, sines = np.cos(angles), np.sin(angles)
        both = np.stack(
            [np.concatenate([cosines, cosines], 1), np.concatenate([sines, -sines], 1)]
        )
        return jnp.asarray((both * scale).astype(np.float32))

    return table(np.arange(rows), 1.0), table(np.arange(blocks) * rows, SCALE)


def local(
    normed_layer_input,
    query,
    saved_key_value,
    output_gradient,
    adapter_down_weight,
    adapter_up_weight,
    shifted_head_flags,
):
    rows, model = normed_layer_input.shape[1:]
    columns = adapter_up_weight.shape[1]
    width = GROUP_HEADS * HD
    row_table, block_table = rotary_constants(rows, lax.axis_size("ctx"))
    dma = pltpu.SemaphoreType.DMA
    grad_proj, grad_down, grad_up, norm = pl.pallas_call(
        kernel,
        out_shape=(
            pltpu.VMEM((rows, columns), BF16),
            jax.ShapeDtypeStruct((3 * ADAPTER_RANK, model // SHARDS), F32),
            jax.ShapeDtypeStruct((ADAPTER_RANK, columns // SHARDS), F32),
            jax.ShapeDtypeStruct((8, HD), F32),
        ),
        in_specs=[HBM] * 9,
        out_specs=(VMEM, VMEM, VMEM, VMEM),
        scratch_shapes=[
            pltpu.SMEM((KVH,), jnp.int32),
            pltpu.VMEM((rows, model), BF16),
            pltpu.VMEM((rows, 2 * KVH * HD), BF16),
            pltpu.VMEM((2 * KVH, rows, HD), BF16),
            pltpu.VMEM((3 * ADAPTER_RANK, model), BF16),
            pltpu.VMEM((ADAPTER_RANK, columns), BF16),
            pltpu.VMEM(row_table.shape, F32),
            pltpu.VMEM(block_table.shape, F32),
            pltpu.VMEM((KVH, rows, width), BF16),
            pltpu.VMEM((KVH, rows, width), BF16),
            pltpu.VMEM((KVH, GROUP_DEV * rows, 2 * HD), BF16),
            pltpu.VMEM((KVH, GROUP_DEV - 1, rows, 2 * HD), BF16),
            pltpu.VMEM((KVH, GROUP_DEV - 1, rows, 2 * HD), BF16),
            pltpu.VMEM((KVH, rows, 2 * HD), F32),
            pltpu.VMEM((KVH, rows, width), BF16),
            pltpu.VMEM((KVH, rows, 2 * HD), BF16),
            pltpu.VMEM((rows, 2 * KVH * HD), BF16),
            pltpu.VMEM((rows, HD), F32),
            pltpu.VMEM((rows, HD), F32),
            pltpu.VMEM((3 * ADAPTER_RANK, rows), F32),
            pltpu.VMEM((ADAPTER_RANK, columns), F32),
            pltpu.VMEM((rows, ADAPTER_RANK), F32),
            pltpu.VMEM((2, SHARDS, PIECE, HD), BF16),
            pltpu.VMEM((SHARDS, PIECE, HD), BF16),
            pltpu.VMEM((SHARDS, PIECE, HD), BF16),
            pltpu.VMEM((PLANE, 2, PIECE, HD), BF16),
            pltpu.VMEM((2, PIECE, HD), F32),
            pltpu.VMEM((RING, 2, PIECE, HD), F32),
            pltpu.VMEM((2, PIECE, HD), F32),
            pltpu.VMEM((PLANE, 8, HD), F32),
            pltpu.VMEM((2, 8, HD), F32),
            dma,
            dma((4,)),
            dma,
            dma,
            dma((2, KVH)),
            dma((KVH, GROUP_DEV - 1)),
            dma((KVH, GROUP_DEV - 1)),
            dma((KVH, GROUP_DEV - 1)),
            dma((KVH, GROUP_DEV - 1)),
            dma((2,)),
            dma((2,)),
            dma((PLANE,)),
            dma((PLANE,)),
            dma((RING,)),
            dma((RING,)),
            dma,
            dma,
            dma((PLANE,)),
            dma((PLANE,)),
            dma,
            dma,
        ],
        compiler_params=pltpu.CompilerParams(
            collective_id=0, has_side_effects=True, vmem_limit_bytes=48 * 2**20
        ),
        name="attention_and_adapter_gradients",
    )(
        *(
            pltpu.with_memory_space_constraint(array, pltpu.HBM)
            for array in (
                shifted_head_flags,
                normed_layer_input[0],
                query[0],
                saved_key_value[0],
                output_gradient[0],
                adapter_down_weight,
                adapter_up_weight,
                row_table,
                block_table,
            )
        ),
    )
    return (grad_proj[None], grad_down, grad_up, norm[0, 0])


def solution(mesh):
    return jax.shard_map(
        local,
        mesh=mesh,
        in_specs=(
            P("dp", "ctx", None),
            P("dp", "ctx", None),
            P("dp", "ctx", None),
            P("dp", "ctx", None),
            P(),
            P(),
            P(),
        ),
        out_specs=(P("dp", "ctx", None), P(None, "ctx"), P(None, "ctx"), P()),
        check_vma=False,
    )
```
